256 devices in a mesh: section: 2 (over z_hi), dp: 4 (over x), expert: 32 (over y, z_lo, core).
Axes of the slice: x: 4, y: 4, z: 8 (z_hi: 2, z_lo: 4; z = z_hi * 4 + z_lo), core: 2. Of those that a mesh axis runs over, the one named last changes fastest.
Arguments:
- activations: bfloat16 [2, 16384, 4096], P('section', ('dp', 'expert')), may hold values from -6 to 6
- norm_gain: float32 [2, 4096], P('section'), may hold values from 0.25 to 1.75
- route_ids: int32 [2, 16384, 2], P('section', ('dp', 'expert')), may hold values from 0 to 15, all different within a row; in each aligned block of 128 rows (0 to 127, 128 to 255, ..., all dimensions but the last counted through in order) at most 18 rows name the same one
- route_gates: float32 [2, 16384, 2], P('section', ('dp', 'expert')), may hold values from 0.2 to 1
- gate_weight: bfloat16 [2, 4096, 12288], P('section', None, 'expert'), may hold values from -0.09375 to 0.09375
- up_weight: bfloat16 [2, 4096, 12288], P('section', None, 'expert'), may hold values from -0.09375 to 0.09375
- leak_rates: float32 [2, 12288], P('section', 'expert'), may hold values from 0.2 to 0.9
- down_weight: bfloat16 [2, 12288, 4096], P('section', 'expert', 'dp'), may hold values from -0.21875 to 0.21875
- cotangent: bfloat16 [2, 16384, 4096], P('section', ('dp', 'expert')), may hold values from -6 to 6
Outputs:
- passed_on: bfloat16 [2, 16384, 4096], P('section', ('dp', 'expert'))
- passed_back: bfloat16 [2, 16384, 4096], P('section', ('dp', 'expert'))
- up_grad: bfloat16 [2, 4096, 12288], P('section', 'dp', 'expert')
The draws below stay inside these ranges and needn't reach their ends.
Inputs may be any that keep to these rules, and one draw needn't show every extreme that they name: `route_ids`: within one section, the 128 tokens of one device name each expert at most 18 times, and some device reaches 18 for some expert; the two experts of a token differ.
All inputs are finite; a program needn't handle non-finite values.
Results may differ from the reference program's by a relative error of at most 0.015.
Values may be sent and summed in bfloat16 or wider, within the bound.
A program may use at most 192 MiB of HBM per device.

```python
import math
import jax
import jax.numpy as jnp
import numpy as np
from jax import lax

D = 4096
FFW = 768
TSTEPS = 4
TOK_DEV = 128
EXPERTS = 16
CAP = 18
TOKENS = 16384
N_SECTION = 2
N_DP = 4
N_EXPERT = 32


def levels(own_key, dims, cuts, low, top_value):
    gain, own = 1.0, jax.random.fold_in(own_key, 6)
    for axis_at, blocks in cuts:
        steps = jnp.exp(jax.random.uniform(jax.random.fold_in(own, axis_at), (blocks,), jnp.float32, low / len(cuts), top_value / len(cuts)))
        gain = gain * jnp.repeat(steps, dims[axis_at] // blocks).reshape([-1 if axis == axis_at else 1 for axis in range(len(dims))])
    return gain


def shared_out(stream_key, own, number, rows, number_of, top, bound, slope):
    sequence = jax.random.permutation(stream_key, number_of)
    heavy_load, common = shares(number_of, rows * top, bound, slope, True), shares(number_of, rows * top, bound, slope, False)
    places = jnp.arange(number_of)

    def named(tallies, offset_by):
        used = int((tallies > 0).sum())
        fixed = max(1, used // 4)
        moved = fixed + (places - fixed + offset_by * (used - fixed)) % max(1, number_of - fixed)
        return jnp.zeros((number_of,), jnp.int32).at[sequence[jnp.where(places < fixed, places, moved)]].set(jnp.asarray(tallies, jnp.int32))

    tallies = jnp.where(number % 4 == 0, named(heavy_load, number // 4), named(common, number - number // 4 - 1))
    mixed = jax.random.permutation(jax.random.fold_in(own, 3), number_of)
    source_of, receiver = mixed[0:number_of // 2 * 2:2], mixed[1:number_of // 2 * 2:2]
    slack = jnp.minimum(tallies[source_of] - 1, bound - tallies[receiver]) // 2
    slack = jnp.where((source_of == sequence[0]) | (receiver == sequence[0]) | (tallies[receiver] == 0), 0, jnp.maximum(slack, 0))
    moved = jax.random.randint(jax.random.fold_in(own, 4), (number_of // 2,), 0, 1 << 20) % (slack + 1)
    tallies = tallies.at[source_of].add(-moved).at[receiver].add(moved)
    members = jnp.searchsorted(jnp.cumsum(tallies), jnp.arange(rows * top), side="right").astype(jnp.int32)
    grid = members.reshape(top, rows).T
    grid = grid[jax.random.permutation(jax.random.fold_in(own, 1), rows)]
    offset_by = jax.random.randint(jax.random.fold_in(own, 2), (rows, 1), 0, top)
    return jnp.take_along_axis(grid, (jnp.arange(top)[None, :] + offset_by) % top, axis=1)


def shares(amount, total, bound, lean, full):
    weights = [(1 << 20) // math.isqrt(grade ** lean) + 1 for grade in range(1, amount + 1)]
    largest = bound if full else min(bound, max(-(-total // amount), total * weights[0] // sum(weights)))
    least = 1 if total - largest >= amount - 1 else 0
    holding, surplus = [largest] + [least] * (amount - 1), total - largest - least * (amount - 1)
    while surplus > 0:
        movable = [i for i in range(1, amount) if holding[i] < largest] or [i for i in range(1, amount) if holding[i] < bound]
        pool, remaining = sum([weights[i] for i in movable]), surplus
        for i in movable:
            addition = min(bound - holding[i], max(1, remaining * weights[i] // pool), surplus)
            holding[i] = holding[i] + addition
            surplus = surplus - addition
    return np.array(holding)


def normal_values(stream_key, shape, scale, limit, pieces=(), kind=jnp.bfloat16):
    drawn = jax.random.normal(stream_key, shape, jnp.float32) * scale
    if len(pieces) > 0:
        drawn = levels(stream_key, shape, pieces, -0.22, 0.18) * drawn
    return jnp.clip(drawn, min=-limit, max=limit).astype(kind)


def setup_inputs(seed: int = 0) -> dict:
    arg_keys = jax.random.split(jax.random.key(seed), 10)
    activations = normal_values(arg_keys[0], (N_SECTION, TOKENS, D), 1.0, 6.0, ((0, 2), (1, 128)))
    norm_gain = jnp.clip(1.0 + 0.15 * jax.random.normal(arg_keys[1], (N_SECTION, D), jnp.float32), 0.25, 1.75)
    route_ids_keys = jax.random.split(jax.random.fold_in(arg_keys[2], 1), N_SECTION * TOKENS // TOK_DEV)
    route_ids_turns = jax.random.permutation(jax.random.fold_in(arg_keys[2], 3), N_SECTION * TOKENS // TOK_DEV)
    route_ids = jax.vmap(lambda own, number: shared_out(jax.random.fold_in(arg_keys[2], 2), own, number, TOK_DEV, EXPERTS, 2, CAP, 2))(route_ids_keys, route_ids_turns).reshape((N_SECTION, TOKENS, 2))
    route_gates = jnp.clip(0.2 + 0.8 * jax.random.uniform(arg_keys[3], (N_SECTION, TOKENS, 2), jnp.float32) ** levels(arg_keys[3], (N_SECTION, TOKENS, 2), ((0, 2), (1, 128)), -0.2, 0.2), 0.2, 1.0)
    gate_weight = normal_values(arg_keys[4], (N_SECTION, D, EXPERTS * FFW), D ** -0.5, 0.09375, ((0, 2), (2, 32)))
    up_weight = normal_values(arg_keys[5], (N_SECTION, D, EXPERTS * FFW), D ** -0.5, 0.09375, ((0, 2), (2, 32)))
    leak_rates = jnp.clip(jnp.exp(math.log(0.9) - 1.50407736 * jax.random.uniform(arg_keys[6], (N_SECTION, EXPERTS * FFW), jnp.float32) ** levels(arg_keys[6], (N_SECTION, EXPERTS * FFW), ((0, 2), (1, 32)), -0.2, 0.2)), 0.2, 0.9)
    down_weight = normal_values(arg_keys[7], (N_SECTION, EXPERTS * FFW, D), FFW ** -0.5, 0.21875, ((0, 2), (1, 32), (2, 4)))
    cotangent = normal_values(arg_keys[8], (N_SECTION, TOKENS, D), 1.0, 6.0, ((0, 2), (1, 128)))
    return dict(activations=activations, norm_gain=norm_gain, route_ids=route_ids, route_gates=route_gates, gate_weight=gate_weight, up_weight=up_weight, leak_rates=leak_rates, down_weight=down_weight, cotangent=cotangent)


EPS = 1e-06
THETA = 0.5
SHARP = 4.0

def lif_rate(gate_act, up_act, leak_rate):
    drive = jax.nn.silu(gate_act) * up_act
    volts = jnp.zeros_like(drive)
    spike_sum = jnp.zeros_like(drive)
    for timestep in range(TSTEPS):
        volts = leak_rate * volts + drive
        spikes = jax.nn.sigmoid(SHARP * (volts - THETA)) - jax.nn.sigmoid(SHARP * (-volts - THETA))
        volts = volts - THETA * spikes
        spike_sum = spike_sum + spikes
    return spike_sum / TSTEPS

def section_pass(tokens_in, gain_row, ids_section, gates_section, gate_section, up_section, leak_section, down_section, grad_section):
    device_count = N_DP * N_EXPERT
    token_count = tokens_in.shape[0]
    tokens = tokens_in.astype(jnp.float32)
    inv_rms = lax.rsqrt(lax.optimization_barrier(jnp.mean(tokens * tokens, axis=-1, keepdims=True)) + EPS)
    normed = (tokens * inv_rms * gain_row).astype(jnp.bfloat16)
    flat_ids = ids_section.reshape(device_count, TOK_DEV * 2)
    onehot = (flat_ids[:, :, None] == jnp.arange(EXPERTS, dtype=jnp.int32)[None, None, :]).astype(jnp.int32)
    slot_index = lax.optimization_barrier(jnp.sum(onehot * (jnp.cumsum(onehot, axis=1) - 1), axis=2))
    places = jnp.arange(device_count, dtype=jnp.int32)[:, None] * CAP + slot_index
    sentinel = token_count * 2
    slot_table = jnp.full((EXPERTS, device_count * CAP), sentinel, jnp.int32)
    slot_table = slot_table.at[flat_ids.reshape(-1), places.reshape(-1)].set(jnp.arange(token_count * 2, dtype=jnp.int32))
    normed_pad = jnp.concatenate([normed, jnp.zeros((1, D), jnp.bfloat16)], axis=0)
    grad_pad = jnp.concatenate([grad_section.astype(jnp.float32), jnp.zeros((1, D), jnp.float32)], axis=0)
    gate_pad = jnp.concatenate([gates_section.reshape(-1).astype(jnp.float32), jnp.zeros((1,), jnp.float32)], axis=0)

    def per_expert(carry, expert):
        moe_sum, input_grad = carry
        route_rows = slot_table[expert]
        token_rows = route_rows // 2
        route_gate = gate_pad[route_rows]
        inputs = normed_pad[token_rows]
        column = (expert * FFW).astype(jnp.int32)
        gate_part = lax.dynamic_slice_in_dim(gate_section, column, FFW, 1)
        up_part = lax.dynamic_slice_in_dim(up_section, column, FFW, 1)
        leak_part = lax.dynamic_slice_in_dim(leak_section, column, FFW, 0)
        down_part = lax.dynamic_slice_in_dim(down_section, column, FFW, 0)
        gate_act = jnp.dot(inputs, gate_part, preferred_element_type=jnp.float32)
        up_act = jnp.dot(inputs, up_part, preferred_element_type=jnp.float32)
        spike_rate = lif_rate(gate_act, up_act, leak_part).astype(jnp.bfloat16)
        expert_out = jnp.dot(spike_rate, down_part, preferred_element_type=jnp.float32).astype(jnp.bfloat16).astype(jnp.float32)
        moe_sum = moe_sum.at[token_rows].add(route_gate[:, None] * expert_out)
        route_grad = (route_gate[:, None] * grad_pad[token_rows]).astype(jnp.bfloat16)
        rate_grad = lax.dot_general(route_grad, down_part, (((1,), (1,)), ((), ())), preferred_element_type=jnp.float32)
        unused_rate, pullback = jax.vjp(lambda gate_in, up_in: lif_rate(gate_in, up_in, leak_part), gate_act, up_act)
        gate_grad, up_act_grad = pullback(rate_grad)
        gate_grad = gate_grad.astype(jnp.bfloat16)
        up_act_grad = up_act_grad.astype(jnp.bfloat16)
        first = lax.dot_general(gate_grad, gate_part, (((1,), (1,)), ((), ())), preferred_element_type=jnp.float32)
        second = lax.dot_general(up_act_grad, up_part, (((1,), (1,)), ((), ())), preferred_element_type=jnp.float32)
        route_back = (first + second).astype(jnp.bfloat16).astype(jnp.float32)
        input_grad = input_grad.at[token_rows].add(route_back)
        grouped = jnp.einsum('grd,grf->gdf', inputs.reshape(N_DP, N_EXPERT * CAP, D).astype(jnp.float32), up_act_grad.reshape(N_DP, N_EXPERT * CAP, FFW).astype(jnp.float32), precision=lax.Precision.HIGHEST)
        expert_grad = lax.optimization_barrier(jnp.sum(grouped.astype(jnp.bfloat16).astype(jnp.float32), axis=0)).astype(jnp.bfloat16)
        return ((moe_sum, input_grad), expert_grad)
    start = (jnp.zeros((token_count + 1, D), jnp.float32), jnp.zeros((token_count + 1, D), jnp.float32))
    (moe_sum, input_grad), expert_grads = lax.scan(per_expert, start, jnp.arange(EXPERTS, dtype=jnp.int32))
    section_out = (tokens + moe_sum[:token_count]).astype(jnp.bfloat16)
    norm_grad = input_grad[:token_count] * gain_row
    section_back = grad_section.astype(jnp.float32) + inv_rms * norm_grad - tokens * (inv_rms * inv_rms * inv_rms) * lax.optimization_barrier(jnp.mean(tokens * norm_grad, axis=-1, keepdims=True))
    up_grad = jnp.transpose(expert_grads, (1, 0, 2)).reshape(D, EXPERTS * FFW)
    return (section_out, section_back.astype(jnp.bfloat16), up_grad)

def reference(activations, norm_gain, route_ids, route_gates, gate_weight, up_weight, leak_rates, down_weight, cotangent):
    outputs = []
    backs = []
    grads = []
    for section_index in range(N_SECTION):
        section_out, section_back, up_grad = section_pass(activations[section_index], norm_gain[section_index], route_ids[section_index], route_gates[section_index], gate_weight[section_index], up_weight[section_index], leak_rates[section_index], down_weight[section_index], cotangent[section_index])
        outputs.append(section_out)
        backs.append(section_back)
        grads.append(up_grad)
    outputs = jnp.stack(outputs)
    backs = jnp.stack(backs)
    passed_on = jnp.concatenate([jnp.zeros_like(outputs[:1]), outputs[:-1]], axis=0)
    passed_back = jnp.concatenate([backs[1:], jnp.zeros_like(backs[:1])], axis=0)
    return (passed_on, passed_back, jnp.stack(grads))
```

```python
import functools

import jax
import jax.numpy as jnp
from jax import lax
from jax.experimental import pallas as pl
from jax.experimental.pallas import tpu as pltpu
from jax.sharding import PartitionSpec as P

MESH = pl.DeviceIdType.MESH
TSTEPS = 4
EPS = 1e-06
THETA = 0.5
SHARP = 4.0
HEAD = 16
TAIL = 2
FOLDS = 8
EXPERTS = 16
F32 = jnp.float32
BF16 = jnp.bfloat16


def iota(shape, dim):
    return lax.broadcasted_iota(jnp.int32, shape, dim)


def dot(a, b):
    return jnp.dot(a, b, preferred_element_type=F32)


def dot_t(a, b):
    return lax.dot_general(a, b, (((1,), (1,)), ((), ())), preferred_element_type=F32)


def t_dot(a, b):
    return lax.dot_general(a, b, (((0,), (0,)), ((), ())), preferred_element_type=F32)


def kernel(
    act_ref, cot_ref, gain_ref, ids_ref, gates_ref, leak_ref, gate_hbm, up_hbm, down_hbm,
    res_ref, upgrad_ref,
    gate_w, up_w, down_w, leak_w,
    send_x, send_xe, send_c, send_ce,
    x_rows, x_ext, c_rows, c_ext,
    gate_act, up_act, rate, der_gate, der_up,
    out_rows, out_ext, back_rows, back_ext,
    total, final,
    own_term, sib_term, sib_recv, rep_recv,
    gg, ug,
    w_own_sem, w_sib_send, w_sib_recv, d_send, d_recv, df_send, df_recv,
    x_send, x_recv, c_send, c_recv, local_sem, b_send, b_recv,
    s_send, s_recv, t_send, t_recv, r_send, r_recv,
):
    sec = lax.axis_index("section")
    dp = lax.axis_index("dp")
    lane = lax.axis_index("expert")
    n_dp = lax.axis_size("dp")
    chip = lane // 2
    core = lane % 2
    tokens, width = act_ref.shape
    fold = width // FOLDS
    rows = EXPERTS * HEAD
    slots = rows + EXPERTS * TAIL
    hidden = gate_hbm.shape[1]
    shard = down_hbm.shape[1]

    def peer(step):
        return (sec, dp, lax.rem(chip + step, EXPERTS) * 2 + core)

    sibling = (sec, dp, chip * 2 + (1 - core))
    across = (1 - sec, dp, lane)

    def replica(step):
        return (sec, lax.rem(dp + step, n_dp), lane)

    def remote(src, dst, send, recv, target):
        return pltpu.make_async_remote_copy(
            src_ref=src, dst_ref=dst, send_sem=send, recv_sem=recv,
            device_id=target, device_id_type=MESH,
        )

    barrier = pltpu.get_barrier_semaphore()

    def greet(step, carry):
        pl.semaphore_signal(barrier, inc=1, device_id=peer(step), device_id_type=MESH)
        return carry

    lax.fori_loop(1, EXPERTS, greet, 0)
    for step in range(1, n_dp):
        pl.semaphore_signal(barrier, inc=1, device_id=replica(step), device_id_type=MESH)
    pl.semaphore_signal(barrier, inc=1, device_id=sibling, device_id_type=MESH)
    pl.semaphore_signal(barrier, inc=1, device_id=across, device_id_type=MESH)
    pl.semaphore_wait(barrier, EXPERTS - 1 + n_dp - 1 + 2)

    own_weights = [
        pltpu.make_async_copy(gate_hbm, gate_w.at[core], w_own_sem.at[0]),
        pltpu.make_async_copy(up_hbm, up_w.at[core], w_own_sem.at[1]),
        pltpu.make_async_copy(down_hbm, down_w.at[core, dp], w_own_sem.at[2]),
        pltpu.make_async_copy(leak_ref, leak_w.at[core], w_own_sem.at[3]),
    ]

    def sib_weights(half):
        return [
            remote(gate_hbm, gate_w.at[half], w_sib_send.at[0], w_sib_recv.at[0], sibling),
            remote(up_hbm, up_w.at[half], w_sib_send.at[1], w_sib_recv.at[1], sibling),
            remote(down_hbm, down_w.at[half, dp], w_sib_send.at[2], w_sib_recv.at[2], sibling),
            remote(leak_ref, leak_w.at[half], w_sib_send.at[3], w_sib_recv.at[3], sibling),
        ]

    for copy in own_weights:
        copy.start()
    for copy in sib_weights(core):
        copy.start()

    def down_copy(step, owner):
        return remote(
            down_hbm, down_w.at[core, owner], d_send.at[step - 1], d_recv.at[step - 1], replica(step)
        )

    for step in range(1, n_dp):
        down_copy(step, dp).start()

    ids = ids_ref[...]
    gates = gates_ref[...]
    named = iota((EXPERTS, tokens), 0)
    first = jnp.where(ids[0:1, :] == named, 1.0, 0.0).astype(F32)
    second = jnp.where(ids[1:2, :] == named, 1.0, 0.0).astype(F32)
    both = first + second
    earlier = jnp.where(iota((tokens, tokens), 0) < iota((tokens, tokens), 1), 1.0, 0.0)
    counts = dot(both.astype(BF16), earlier.astype(BF16))
    gate_of = first * gates[0:1, :] + second * gates[1:2, :]
    spread = jnp.where(iota((rows, EXPERTS), 0) // HEAD == iota((rows, EXPERTS), 1), 1.0, 0.0)
    spread16 = spread.astype(BF16)
    both_x = dot(spread16, both.astype(BF16))
    counts_x = dot(spread16, counts.astype(BF16))
    gate_x = jnp.dot(spread, gate_of, precision=lax.Precision.HIGHEST, preferred_element_type=F32)
    row_at = iota((rows, tokens), 0)
    head = both_x * jnp.where(counts_x == (row_at % HEAD).astype(F32), 1.0, 0.0)
    tail = both_x * jnp.where(counts_x == (HEAD + row_at % TAIL).astype(F32), 1.0, 0.0)
    fold_at = (row_at % HEAD) // TAIL
    head_gate = jnp.sum(head * gate_x, axis=1, keepdims=True)
    tail_gate = jnp.sum(tail * gate_x, axis=1, keepdims=True)
    head16 = head.astype(BF16)

    acts = act_ref[...].astype(F32)
    inv_rms = lax.rsqrt(jnp.mean(acts * acts, axis=-1, keepdims=True) + EPS)

    def columns(at):
        return pl.ds(pl.multiple_of(at * fold, fold), fold)

    def prepare(at, carry):
        cols = columns(at)
        normed = (act_ref[:, cols].astype(F32) * inv_rms * gain_ref[:, cols]).astype(BF16)
        send_x[:, cols] = dot(head16, normed).astype(BF16)
        part = jnp.where(fold_at == at, tail, 0.0).astype(BF16)
        return carry + dot(part, normed)

    ext = lax.fori_loop(0, FOLDS, prepare, jnp.zeros((rows, fold), F32))
    send_xe[...] = ext.astype(BF16)

    def block(at):
        return pl.ds(pl.multiple_of(at * HEAD, HEAD), HEAD)

    def exchange(src, dst, ext_src, ext_dst, send, recv, step, there, landed):
        return (
            remote(src.at[block(there), :], dst.at[block(landed), :], send.at[step], recv.at[step], peer(step)),
            remote(
                ext_src.at[block(there), :], ext_dst.at[block(landed), :],
                send.at[EXPERTS + step], recv.at[EXPERTS + step], peer(step),
            ),
        )

    def send_all(src, dst, ext_src, ext_dst, send, recv):
        def body(step, carry):
            there = lax.rem(chip + step, EXPERTS)
            for copy in exchange(src, dst, ext_src, ext_dst, send, recv, step, there, chip):
                copy.start()
            return carry

        lax.fori_loop(1, EXPERTS, body, 0)

    def wait_all(src, dst, ext_src, ext_dst, send, recv):
        def body(step, carry):
            origin = lax.rem(chip + EXPERTS - step, EXPERTS)
            for copy in exchange(src, dst, ext_src, ext_dst, send, recv, step, origin, origin):
                copy.wait_recv()
            return carry

        lax.fori_loop(1, EXPERTS, body, 0)

    def wait_sent(src, dst, ext_src, ext_dst, send, recv):
        def body(step, carry):
            there = lax.rem(chip + step, EXPERTS)
            for copy in exchange(src, dst, ext_src, ext_dst, send, recv, step, there, chip):
                copy.wait_send()
            return carry

        lax.fori_loop(1, EXPERTS, body, 0)

    def keep_own(src, dst, ext_src, ext_dst):
        dst[block(chip), :] = src[block(chip), :]
        ext_dst[block(chip), :] = ext_src[block(chip), :]

    x_way = (send_x, x_rows, send_xe, x_ext)
    c_way = (send_c, c_rows, send_ce, c_ext)
    b_way = (out_rows, back_rows, out_ext, back_ext)
    send_all(*x_way, x_send, x_recv)
    keep_own(*x_way)

    def prepare_grad(at, carry):
        cols = columns(at)
        upstream = cot_ref[:, cols]
        send_c[:, cols] = (dot(head16, upstream) * head_gate).astype(BF16)
        part = jnp.where(fold_at == at, tail, 0.0).astype(BF16)
        return carry + dot(part, upstream)

    ext = lax.fori_loop(0, FOLDS, prepare_grad, jnp.zeros((rows, fold), F32))
    send_ce[...] = (ext * tail_gate).astype(BF16)
    send_all(*c_way, c_send, c_recv)
    keep_own(*c_way)

    for copy in own_weights:
        copy.wait()
    for copy in sib_weights(1 - core):
        copy.wait_recv()
    for copy in sib_weights(core):
        copy.wait_send()

    def forward_down(step, half, owner):
        return remote(
            down_w.at[core, owner], down_w.at[half, owner],
            df_send.at[step - 1], df_recv.at[step - 1], sibling,
        )

    for step in range(1, n_dp):
        owner = lax.rem(dp + n_dp - step, n_dp)
        down_copy(step, owner).wait_recv()
        forward_down(step, core, owner).start()
    for step in range(1, n_dp):
        owner = lax.rem(dp + n_dp - step, n_dp)
        forward_down(step, 1 - core, owner).wait_recv()
        forward_down(step, core, owner).wait_send()
        down_copy(step, dp).wait_send()

    unfold_row = iota((EXPERTS * TAIL, rows), 0)
    unfold_col = iota((EXPERTS * TAIL, rows), 1)
    same = jnp.logical_and(
        unfold_row // TAIL == unfold_col // HEAD, unfold_row % TAIL == unfold_col % TAIL
    )
    unfold = jnp.where(same, 1.0, 0.0)
    unfold_at = (unfold_col % HEAD) // TAIL
    refold_row = iota((rows, EXPERTS * TAIL), 0)
    refold_col = iota((rows, EXPERTS * TAIL), 1)
    alike = jnp.logical_and(
        refold_col // TAIL == refold_row // HEAD, refold_col % TAIL == refold_row % TAIL
    )
    refold = jnp.where(alike, 1.0, 0.0)
    refold_at = (refold_row % HEAD) // TAIL

    def unfold_tail(ext_ref, rows_ref):
        def body(at, carry):
            pick = jnp.where(unfold_at == at, unfold, 0.0).astype(BF16)
            rows_ref[rows:slots, columns(at)] = dot(pick, ext_ref[...]).astype(BF16)
            return carry

        lax.fori_loop(0, FOLDS, body, 0)

    wait_all(*x_way, x_send, x_recv)
    unfold_tail(x_ext, x_rows)

    for half in range(2):
        gate_act[half] = jnp.zeros((slots, hidden), F32)
        up_act[half] = jnp.zeros((slots, hidden), F32)

        def project(at, carry):
            cols = columns(at)
            gate_act[half] += dot(x_rows[:, cols], gate_w[half, cols, :])
            up_act[half] += dot(x_rows[:, cols], up_w[half, cols, :])
            return carry

        lax.fori_loop(0, FOLDS, project, 0)

        def spiking(at, carry):
            part = pl.ds(pl.multiple_of(at * 32, 32), 32)
            gate_in = gate_act[half, part, :]
            up_in = up_act[half, part, :]
            leak = leak_w[half, 0:1, :]
            opened = lax.logistic(gate_in)
            silu = gate_in * opened
            drive = silu * up_in
            volts = drive
            volts_d = jnp.ones_like(drive)
            spike_sum = jnp.zeros_like(drive)
            spike_d = jnp.zeros_like(drive)
            for timestep in range(TSTEPS):
                if timestep:
                    volts = leak * volts + drive
                    volts_d = leak * volts_d + 1.0
                plus = lax.logistic(SHARP * (volts - THETA))
                minus = lax.logistic(SHARP * (-volts - THETA))
                spikes = plus - minus
                slope = SHARP * (plus * (1.0 - plus) + minus * (1.0 - minus))
                spikes_d = slope * volts_d
                volts = volts - THETA * spikes
                volts_d = volts_d - THETA * spikes_d
                spike_sum = spike_sum + spikes
                spike_d = spike_d + spikes_d
            rate[half, part, :] = (spike_sum / TSTEPS).astype(BF16)
            drive_d = spike_d / TSTEPS
            der_gate[half, part, :] = drive_d * up_in * (opened * (1.0 + gate_in * (1.0 - opened)))
            der_up[half, part, :] = drive_d * silu
            return carry

        lax.fori_loop(0, slots // 32, spiking, 0)

    def fold_tail():
        def body(at, carry):
            pick = jnp.where(refold_at == at, refold, 0.0).astype(BF16)
            return carry + dot(pick, out_rows[rows:slots, columns(at)])

        out_ext[...] = lax.fori_loop(0, FOLDS, body, jnp.zeros((rows, fold), F32)).astype(BF16)

    @pl.when(sec == 0)
    def _():
        for owner in range(n_dp):
            out_rows[:, owner * shard : (owner + 1) * shard] = (
                dot(rate[0], down_w[0, owner]) + dot(rate[1], down_w[1, owner])
            ).astype(BF16)
        fold_tail()
        send_all(*b_way, b_send, b_recv)
        keep_own(*b_way)

    wait_all(*c_way, c_send, c_recv)
    unfold_tail(c_ext, c_rows)
    for half in range(2):
        rate_grad = jnp.zeros((slots, hidden), F32)
        for owner in range(n_dp):
            rate_grad = rate_grad + dot_t(
                c_rows[:, owner * shard : (owner + 1) * shard], down_w[half, owner]
            )
        gg[half] = (rate_grad * der_gate[half]).astype(BF16)
        ug[half] = (rate_grad * der_up[half]).astype(BF16)

    @pl.when(sec == 1)
    def _():
        def body(at, carry):
            cols = columns(at)
            out_rows[:, cols] = (
                dot_t(gg[0], gate_w[0, cols, :]) + dot_t(gg[1], gate_w[1, cols, :])
                + dot_t(ug[0], up_w[0, cols, :]) + dot_t(ug[1], up_w[1, cols, :])
            ).astype(BF16)
            return carry

        lax.fori_loop(0, FOLDS, body, 0)
        fold_tail()
        send_all(*b_way, b_send, b_recv)
        keep_own(*b_way)

    def sib_copy(step, at):
        part = pl.ds(pl.multiple_of(at * shard, shard), shard)
        return remote(sib_term.at[part, :], sib_recv.at[part, :], t_send.at[step], t_recv.at[step], sibling)

    def rep_copy(step, at):
        part = pl.ds(pl.multiple_of(at * shard, shard), shard)
        return remote(
            sib_recv.at[part, :], rep_recv.at[step - 1], r_send.at[step - 1], r_recv.at[step - 1], replica(step)
        )

    halves = shard // 2
    for step in range(n_dp + 1):
        if step < n_dp:
            at = lax.rem(dp + step + 1, n_dp)
            for piece in range(2):
                low = piece * halves
                part = pl.ds(pl.multiple_of(at * shard + low, halves), halves)
                own_term[step % 2, low : low + halves, :] = t_dot(x_rows[:, part], ug[core])
                sib_term[part, :] = t_dot(x_rows[:, part], ug[1 - core]).astype(BF16)
            sib_copy(step, at).start()
        if step > 0:
            at = lax.rem(dp + step, n_dp)
            sib_copy(step - 1, at).wait()
            part = pl.ds(pl.multiple_of(at * shard, shard), shard)
            sib_recv[part, :] = (own_term[(step - 1) % 2] + sib_recv[part, :].astype(F32)).astype(BF16)
            if step < n_dp:
                rep_copy(step, at).start()

    wait_all(*b_way, b_send, b_recv)

    def pass_copy(at):
        return remote(
            final.at[:, columns(at)], res_ref.at[:, columns(at)], s_send.at[at], s_recv.at[at], across
        )

    is_first = sec == 0
    head_mix = jnp.where(is_first, head * gate_x, head).T.astype(BF16)
    tail_mix = jnp.where(is_first, tail * gate_x, tail).T
    fold_t = (iota((tokens, rows), 1) % HEAD) // TAIL

    def mixed(at):
        cols = columns(at)
        part = jnp.where(fold_t == at, tail_mix, 0.0).astype(BF16)
        return dot(head_mix, back_rows[:, cols]) + dot(part, back_ext[...])

    @pl.when(sec == 0)
    def _():
        def body(at, carry):
            cols = columns(at)
            final[:, cols] = (act_ref[:, cols].astype(F32) + mixed(at)).astype(BF16)
            pass_copy(at).start()
            return carry

        lax.fori_loop(0, FOLDS, body, 0)

    @pl.when(sec == 1)
    def _():
        def gather(at, carry):
            cols = columns(at)
            norm_grad = mixed(at) * gain_ref[:, cols]
            total[:, cols] = norm_grad
            return carry + jnp.sum(act_ref[:, cols].astype(F32) * norm_grad, axis=-1, keepdims=True)

        mean = lax.fori_loop(0, FOLDS, gather, jnp.zeros((tokens, 1), F32)) / width
        scale = inv_rms * inv_rms * inv_rms * mean

        def body(at, carry):
            cols = columns(at)
            final[:, cols] = (
                cot_ref[:, cols].astype(F32)
                + inv_rms * total[:, cols]
                - act_ref[:, cols].astype(F32) * scale
            ).astype(BF16)
            pass_copy(at).start()
            return carry

        lax.fori_loop(0, FOLDS, body, 0)

    for step in range(1, n_dp):
        rep_copy(step, dp).wait_recv()
    own = pl.ds(pl.multiple_of(dp * shard, shard), shard)
    total_grad = sib_recv[own, :].astype(F32)
    for step in range(1, n_dp):
        total_grad = total_grad + rep_recv[step - 1].astype(F32)
    upgrad_ref[...] = total_grad.astype(BF16)

    wait_sent(*x_way, x_send, x_recv)
    wait_sent(*c_way, c_send, c_recv)
    wait_sent(*b_way, b_send, b_recv)
    for step in range(1, n_dp):
        rep_copy(step, dp).wait_send()

    def finish(at, carry):
        pass_copy(at).wait()
        return carry

    lax.fori_loop(0, FOLDS, finish, 0)


def per_device(
    activations, norm_gain, route_ids, route_gates, gate_weight, up_weight, leak_rates, down_weight, cotangent
):
    tokens, width = activations.shape[1:]
    hidden = gate_weight.shape[2]
    shard = down_weight.shape[2]
    n_dp = lax.axis_size("dp")
    rows = EXPERTS * HEAD
    slots = rows + EXPERTS * TAIL
    fold = width // FOLDS
    vmem = pl.BlockSpec(memory_space=pltpu.VMEM)
    anywhere = pl.BlockSpec(memory_space=pl.ANY)
    dma = pltpu.SemaphoreType.DMA

    def scratch(kind, *shape):
        return pltpu.VMEM(shape, kind)

    result, up_grad = pl.pallas_call(
        kernel,
        out_shape=(
            jax.ShapeDtypeStruct((tokens, width), BF16),
            jax.ShapeDtypeStruct((shard, hidden), BF16),
        ),
        in_specs=[vmem] * 6 + [anywhere] * 3,
        out_specs=(anywhere, vmem),
        scratch_shapes=[
            scratch(BF16, 2, width, hidden),
            scratch(BF16, 2, width, hidden),
            scratch(BF16, 2, n_dp, hidden, shard),
            scratch(F32, 2, 8, hidden),
            scratch(BF16, rows, width),
            scratch(BF16, rows, fold),
            scratch(BF16, rows, width),
            scratch(BF16, rows, fold),
            scratch(BF16, slots, width),
            scratch(BF16, rows, fold),
            scratch(BF16, slots, width),
            scratch(BF16, rows, fold),
            scratch(F32, 2, slots, hidden),
            scratch(F32, 2, slots, hidden),
            scratch(BF16, 2, slots, hidden),
            scratch(F32, 2, slots, hidden),
            scratch(F32, 2, slots, hidden),
            scratch(BF16, slots, width),
            scratch(BF16, rows, fold),
            scratch(BF16, rows, width),
            scratch(BF16, rows, fold),
            scratch(F32, tokens, width),
            scratch(BF16, tokens, width),
            scratch(F32, 2, shard, hidden),
            scratch(BF16, width, hidden),
            scratch(BF16, width, hidden),
            scratch(BF16, n_dp - 1, shard, hidden),
            scratch(BF16, 2, slots, hidden),
            scratch(BF16, 2, slots, hidden),
            dma((4,)), dma((4,)), dma((4,)),
            dma((n_dp - 1,)), dma((n_dp - 1,)), dma((n_dp - 1,)), dma((n_dp - 1,)),
            dma((2 * EXPERTS,)), dma((2 * EXPERTS,)), dma((2 * EXPERTS,)), dma((2 * EXPERTS,)),
            dma((1,)), dma((2 * EXPERTS,)), dma((2 * EXPERTS,)),
            dma((FOLDS,)), dma((FOLDS,)), dma((n_dp,)), dma((n_dp,)),
            dma((n_dp - 1,)), dma((n_dp - 1,)),
        ],
        compiler_params=pltpu.CompilerParams(
            collective_id=0, has_side_effects=True, vmem_limit_bytes=60 * 2**20
        ),
    )(
        activations[0],
        cotangent[0],
        norm_gain,
        route_ids[0].T,
        route_gates[0].T,
        jnp.broadcast_to(leak_rates, (8, hidden)),
        gate_weight[0],
        up_weight[0],
        down_weight[0],
    )
    first = lax.axis_index("section") == 0
    nothing = jnp.zeros_like(result)
    passed_on = jnp.where(first, nothing, result)
    passed_back = jnp.where(first, result, nothing)
    return (passed_on[None], passed_back[None], up_grad[None])


def solution(mesh):
    return jax.shard_map(
        per_device,
        mesh=mesh,
        in_specs=(
            P("section", ("dp", "expert"), None),
            P("section", None),
            P("section", ("dp", "expert"), None),
            P("section", ("dp", "expert"), None),
            P("section", None, "expert"),
            P("section", None, "expert"),
            P("section", "expert"),
            P("section", "expert", "dp"),
            P("section", ("dp", "expert"), None),
        ),
        out_specs=(
            P("section", ("dp", "expert"), None),
            P("section", ("dp", "expert"), None),
            P("section", "dp", "expert"),
        ),
        check_vma=False,
    )
```

```python
import functools

import jax
import jax.numpy as jnp
from jax import lax
from jax.experimental import pallas as pl
from jax.experimental.pallas import tpu as pltpu
from jax.sharding import PartitionSpec as P

MESH = pl.DeviceIdType.MESH
TSTEPS = 4
EPS = 1e-06
THETA = 0.5
SHARP = 4.0
HEAD = 16
TAIL = 2
FOLDS = 8
LANES = 128
QUARTERS = 4
EXPERTS = 16
RUN = 4
F32 = jnp.float32
BF16 = jnp.bfloat16


def iota(shape, dim):
    return lax.broadcasted_iota(jnp.int32, shape, dim)


def dot(a, b):
    return jnp.dot(a, b, preferred_element_type=F32)


def dot_t(a, b):
    return lax.dot_general(a, b, (((1,), (1,)), ((), ())), preferred_element_type=F32)


def t_dot(a, b):
    return lax.dot_general(a, b, (((0,), (0,)), ((), ())), preferred_element_type=F32)


def folds(value):
    return jnp.concatenate([value[:, at * LANES : (at + 1) * LANES] for at in range(FOLDS)], axis=0)


def fold_order(blocks, inverse):
    size = blocks * HEAD
    by_fold, by_block = iota((size, size), int(inverse)), iota((size, size), 1 - int(inverse))
    match = jnp.logical_and(
        by_fold // (blocks * TAIL) == (by_block % HEAD) // TAIL,
        jnp.logical_and(
            (by_fold % (blocks * TAIL)) // TAIL == by_block // HEAD, by_fold % TAIL == by_block % TAIL
        ),
    )
    return jnp.where(match, 1.0, 0.0).astype(BF16)


def routes(ids, tokens):
    named = iota((EXPERTS, tokens), 0).astype(F32)
    first = jnp.where(ids[0:1, :] == named, 1.0, 0.0)
    second = jnp.where(ids[1:2, :] == named, 1.0, 0.0)
    both = first + second
    earlier = jnp.where(iota((tokens, tokens), 0) < iota((tokens, tokens), 1), 1.0, 0.0)
    counts = dot(both.astype(BF16), earlier.astype(BF16))
    return first, second, both, counts


def slots_of(expert_at, slot_at, both, counts, weights):
    spread = jnp.where(expert_at[:, :EXPERTS] == iota((expert_at.shape[0], EXPERTS), 1), 1.0, 0.0)
    both_x = dot(spread.astype(BF16), both.astype(BF16))
    counts_x = dot(spread.astype(BF16), counts.astype(BF16))
    weights_x = jnp.dot(spread, weights, precision=lax.Precision.HIGHEST, preferred_element_type=F32)
    taken = both_x * jnp.where(counts_x == slot_at.astype(F32), 1.0, 0.0)
    return taken, taken * weights_x


def kernel(
    act_ref, cot_ref, gain_ref, ids_ref, gates_ref, leak_ref, gate_hbm, up_hbm, down_hbm,
    res_ref, upgrad_ref,
    gate_w, up_w, down_w, leak_w,
    send_x, send_xe, send_c, send_ce,
    x_rows, x_ext, c_rows, c_ext,
    gate_act, up_act, rate, der_gate, der_up, rate_grad,
    out_rows, out_ext, back_rows, back_ext, far_rows, far_ext,
    final, landed, meta, meta_recv, dots, dots_recv, mix, far_mix,
    own_term, sib_term, sib_recv, rep_recv,
    gg, ug,
    w_own_sem, w_sib_send, w_sib_recv, d_send, d_recv, df_send, df_recv,
    x_send, x_recv, c_send, c_recv, b_send, b_recv, f_recv,
    s_send, s_recv, t_send, t_recv, r_send, r_recv, m_send, m_recv, v_send, v_recv,
):
    sec = lax.axis_index("section")
    dp = lax.axis_index("dp")
    lane = lax.axis_index("expert")
    n_dp = lax.axis_size("dp")
    chip = lane // 2
    core = lane % 2
    depth = chip % RUN
    tokens, width = act_ref.shape
    quarter = width // QUARTERS
    rows = EXPERTS * HEAD
    slots = rows + EXPERTS * TAIL
    hidden = gate_hbm.shape[1]
    shard = down_hbm.shape[1]
    far_blocks = EXPERTS // 2
    far_heads = far_blocks * HEAD
    far_slots = far_heads + far_blocks * TAIL

    def peer(step, section=sec):
        return (section, dp, lax.rem(chip + step, EXPERTS) * 2 + core)

    sibling = (sec, dp, chip * 2 + (1 - core))
    across = (1 - sec, dp, lane)

    def replica(step):
        return (sec, lax.rem(dp + step, n_dp), lane)

    def at_edge(place):
        return ((place + 1) // 2 + 1) % 2

    def is_far(home, expert):
        home_at, expert_at = home % RUN, expert % RUN
        return at_edge(home_at) * ((home_at // 2 + expert_at // 2) % 2)

    def remote(src, dst, send, recv, target):
        return pltpu.make_async_remote_copy(
            src_ref=src, dst_ref=dst, send_sem=send, recv_sem=recv,
            device_id=target, device_id_type=MESH,
        )

    barrier = pltpu.get_barrier_semaphore()

    def greet(step, carry):
        pl.semaphore_signal(barrier, inc=1, device_id=peer(step), device_id_type=MESH)
        pl.semaphore_signal(barrier, inc=1, device_id=peer(step, 1 - sec), device_id_type=MESH)
        return carry

    lax.fori_loop(1, EXPERTS, greet, 0)
    for step in range(1, n_dp):
        pl.semaphore_signal(barrier, inc=1, device_id=replica(step), device_id_type=MESH)
    pl.semaphore_signal(barrier, inc=1, device_id=sibling, device_id_type=MESH)
    pl.semaphore_signal(barrier, inc=1, device_id=across, device_id_type=MESH)

    ids = ids_ref[...].astype(F32)
    gates = gates_ref[...]
    first, second, both, counts = routes(ids, tokens)
    gate_of = first * gates[0:1, :] + second * gates[1:2, :]
    row_at = iota((slots, tokens), 0)
    in_head = row_at < rows
    expert_at = jnp.where(in_head, row_at // HEAD, (row_at - rows) // TAIL)
    slot_at = jnp.where(in_head, row_at % HEAD, HEAD + row_at % TAIL)
    taken, taken_gate = slots_of(expert_at, slot_at, both, counts, gate_of)
    slot_gate = jnp.sum(taken_gate, axis=1, keepdims=True)
    pick = taken.astype(BF16)
    fold_up = fold_order(EXPERTS, True)
    unfold_all = fold_order(EXPERTS, False)

    acts = act_ref[...].astype(F32)
    inv_rms = lax.rsqrt(jnp.mean(acts * acts, axis=-1, keepdims=True) + EPS)

    def columns(at):
        return slice(at * quarter, (at + 1) * quarter)

    def lanes(at):
        return slice(at * LANES, (at + 1) * LANES)

    def block(at):
        return pl.ds(pl.multiple_of(at * HEAD, HEAD), HEAD)

    def store_slots(at, value, head_ref, ext_ref):
        head_ref[0:rows, columns(at)] = value[0:rows].astype(BF16)
        ext_ref[:, lanes(at)] = dot(fold_up, folds(value[rows:slots].astype(BF16))).astype(BF16)

    def unfold(at, head_ref, ext_ref, order, heads, tails):
        back = dot(order, ext_ref[:, lanes(at)]).astype(BF16)
        for fold in range(FOLDS):
            low = at * quarter + fold * LANES
            head_ref[heads : heads + tails, low : low + LANES] = back[fold * tails : (fold + 1) * tails]

    def pieces(way, sems, at, step, there, landed_at):
        src, dst, ext_src, ext_dst = way
        send, recv = sems
        return (
            remote(
                src.at[block(there), columns(at)], dst.at[block(landed_at), columns(at)],
                send.at[at, step], recv.at[at, step], peer(step),
            ),
            remote(
                ext_src.at[block(there), lanes(at)], ext_dst.at[block(landed_at), lanes(at)],
                send.at[at, EXPERTS + step], recv.at[at, EXPERTS + step], peer(step),
            ),
        )

    def send_all(way, sems, at):
        def body(step, carry):
            for copy in pieces(way, sems, at, step, lax.rem(chip + step, EXPERTS), chip):
                copy.start()
            return carry

        lax.fori_loop(1, EXPERTS, body, 0)

    def wait_all(way, sems, at):
        def body(step, carry):
            origin = lax.rem(chip + EXPERTS - step, EXPERTS)
            for copy in pieces(way, sems, at, step, origin, origin):
                copy.wait_recv()
            return carry

        lax.fori_loop(1, EXPERTS, body, 0)

    def wait_sent(way, sems):
        for at in range(QUARTERS):

            def body(step, carry):
                for copy in pieces(way, sems, at, step, lax.rem(chip + step, EXPERTS), chip):
                    copy.wait_send()
                return carry

            lax.fori_loop(1, EXPERTS, body, 0)

    def keep_own(way, at):
        src, dst, ext_src, ext_dst = way
        dst[block(chip), columns(at)] = src[block(chip), columns(at)]
        ext_dst[block(chip), lanes(at)] = ext_src[block(chip), lanes(at)]

    x_way, x_sems = (send_x, x_rows, send_xe, x_ext), (x_send, x_recv)
    c_way, c_sems = (send_c, c_rows, send_ce, c_ext), (c_send, c_recv)
    b_way, b_sems = (out_rows, back_rows, out_ext, back_ext), (b_send, b_recv)

    own_weights = [
        pltpu.make_async_copy(gate_hbm, gate_w.at[core], w_own_sem.at[0]),
        pltpu.make_async_copy(up_hbm, up_w.at[core], w_own_sem.at[1]),
        pltpu.make_async_copy(down_hbm, down_w.at[core, dp], w_own_sem.at[2]),
        pltpu.make_async_copy(leak_ref, leak_w.at[core], w_own_sem.at[3]),
    ]

    def sib_weights(half):
        return [
            remote(gate_hbm, gate_w.at[half], w_sib_send.at[0], w_sib_recv.at[0], sibling),
            remote(up_hbm, up_w.at[half], w_sib_send.at[1], w_sib_recv.at[1], sibling),
            remote(down_hbm, down_w.at[half, dp], w_sib_send.at[2], w_sib_recv.at[2], sibling),
            remote(leak_ref, leak_w.at[half], w_sib_send.at[3], w_sib_recv.at[3], sibling),
        ]

    def down_copy(step, owner):
        return remote(
            down_hbm, down_w.at[core, owner], d_send.at[step - 1], d_recv.at[step - 1], replica(step)
        )

    def meta_copy():
        return remote(meta, meta_recv, m_send.at[0], m_recv.at[0], across)

    def prepare(at):
        cols = columns(at)
        normed = (act_ref[:, cols].astype(F32) * inv_rms * gain_ref[:, cols]).astype(BF16)
        store_slots(at, dot(pick, normed), send_x, send_xe)

    prepare(0)
    pl.semaphore_wait(barrier, 2 * (EXPERTS - 1) + n_dp - 1 + 2)
    send_all(x_way, x_sems, 0)

    for copy in own_weights:
        copy.start()
    for copy in sib_weights(core):
        copy.start()
    for step in range(1, n_dp):
        down_copy(step, dp).start()

    for at in range(1, QUARTERS):
        prepare(at)
        send_all(x_way, x_sems, at)
    for at in range(QUARTERS):
        store_slots(at, dot(pick, cot_ref[:, columns(at)]) * slot_gate, send_c, send_ce)
        send_all(c_way, c_sems, at)
    for at in range(QUARTERS):
        keep_own(x_way, at)
        keep_own(c_way, at)

    one = jnp.where(iota((tokens, tokens), 0) == iota((tokens, tokens), 1), 1.0, 0.0)
    inv_row = jnp.sum(one * inv_rms, axis=0, keepdims=True)
    is_first = sec == 0
    meta[...] = jnp.zeros_like(meta)
    meta[0:2, :] = ids
    meta[2:3, :] = jnp.where(is_first, gates[0:1, :], inv_row)
    meta[3:4, :] = jnp.where(is_first, gates[1:2, :], inv_row)
    meta_copy().start()

    differs = jnp.where((expert_at % RUN) // 2 == depth // 2, 0.0, 1.0) * at_edge(depth).astype(F32)
    mix[...] = (jnp.where(is_first, taken_gate, taken * inv_row) * (1.0 - differs)).T.astype(BF16)

    def clear(origin, carry):
        @pl.when(is_far(chip, origin) == 1)
        def _():
            back_rows[block(origin), :] = jnp.zeros((HEAD, width), BF16)
            back_ext[block(origin), :] = jnp.zeros((HEAD, QUARTERS * LANES), BF16)

        return carry

    lax.fori_loop(0, EXPERTS, clear, 0)

    for copy in own_weights:
        copy.wait()
    for copy in sib_weights(1 - core):
        copy.wait_recv()
    for copy in sib_weights(core):
        copy.wait_send()

    for at in range(QUARTERS):
        wait_all(x_way, x_sems, at)
        unfold(at, x_rows, x_ext, unfold_all, rows, slots - rows)
        for half in range(2):
            for weight, total in ((gate_w, gate_act), (up_w, up_act)):
                part = dot(x_rows[:, columns(at)], weight[half, columns(at), :])
                total[half] = part if at == 0 else total[half] + part

    for half in range(2):

        def spiking(at, carry):
            part = pl.ds(pl.multiple_of(at * 32, 32), 32)
            gate_in = gate_act[half, part, :]
            up_in = up_act[half, part, :]
            leak = leak_w[half, 0:1, :]
            opened = lax.logistic(gate_in)
            silu = gate_in * opened
            drive = silu * up_in
            volts = drive
            volts_d = jnp.ones_like(drive)
            spike_sum = jnp.zeros_like(drive)
            spike_d = jnp.zeros_like(drive)
            for timestep in range(TSTEPS):
                if timestep:
                    volts = leak * volts + drive
                    volts_d = leak * volts_d + 1.0
                plus = lax.logistic(SHARP * (volts - THETA))
                minus = lax.logistic(SHARP * (-volts - THETA))
                spikes = plus - minus
                slope = SHARP * (plus * (1.0 - plus) + minus * (1.0 - minus))
                spikes_d = slope * volts_d
                volts = volts - THETA * spikes
                volts_d = volts_d - THETA * spikes_d
                spike_sum = spike_sum + spikes
                spike_d = spike_d + spikes_d
            rate[half, part, :] = (spike_sum / TSTEPS).astype(BF16)
            drive_d = spike_d / TSTEPS
            der_gate[half, part, :] = drive_d * up_in * (opened * (1.0 + gate_in * (1.0 - opened)))
            der_up[half, part, :] = drive_d * silu
            return carry

        lax.fori_loop(0, slots // 32, spiking, 0)

    def forward_down(step, half, owner):
        return remote(
            down_w.at[core, owner], down_w.at[half, owner],
            df_send.at[step - 1], df_recv.at[step - 1], sibling,
        )

    for step in range(1, n_dp):
        owner = lax.rem(dp + n_dp - step, n_dp)
        down_copy(step, owner).wait_recv()
        forward_down(step, core, owner).start()
    for step in range(1, n_dp):
        owner = lax.rem(dp + n_dp - step, n_dp)
        forward_down(step, 1 - core, owner).wait_recv()
        forward_down(step, core, owner).wait_send()
        down_copy(step, dp).wait_send()

    def far_place(origin):
        return (origin // RUN) * 2 + origin % 2

    def far_pieces(at, step, there, place):
        return (
            remote(
                out_rows.at[block(there), columns(at)], far_rows.at[block(place), columns(at)],
                b_send.at[at, step], f_recv.at[at, place], peer(step, 1 - sec),
            ),
            remote(
                out_ext.at[block(there), lanes(at)], far_ext.at[block(place), lanes(at)],
                b_send.at[at, EXPERTS + step], f_recv.at[at, far_blocks + place], peer(step, 1 - sec),
            ),
        )

    def send_back(at):
        def body(step, carry):
            there = lax.rem(chip + step, EXPERTS)
            far = is_far(there, chip)

            @pl.when(far == 0)
            def _():
                for copy in pieces(b_way, b_sems, at, step, there, chip):
                    copy.start()

            @pl.when(far == 1)
            def _():
                for copy in far_pieces(at, step, there, far_place(chip)):
                    copy.start()

            return carry

        lax.fori_loop(1, EXPERTS, body, 0)
        keep_own(b_way, at)

    def wait_near(at):
        def body(step, carry):
            origin = lax.rem(chip + EXPERTS - step, EXPERTS)

            @pl.when(is_far(chip, origin) == 0)
            def _():
                for copy in pieces(b_way, b_sems, at, step, origin, origin):
                    copy.wait_recv()

            return carry

        lax.fori_loop(1, EXPERTS, body, 0)

    def wait_far(at):
        def body(place, carry):
            for copy in far_pieces(at, 1, 0, place):
                copy.wait_recv()
            return carry

        lax.fori_loop(0, far_blocks, body, 0)

    @pl.when(sec == 0)
    def _():
        for at in range(QUARTERS):
            value = dot(rate[0], down_w[0, at]) + dot(rate[1], down_w[1, at])
            store_slots(at, value, out_rows, out_ext)
            send_back(at)

    meta_copy().wait()
    far_first, far_second, far_both, far_counts = routes(meta_recv[0:2, :], tokens)
    far_weights = far_first * meta_recv[2:3, :] + far_second * meta_recv[3:4, :]
    far_row = iota((far_slots, tokens), 0)
    far_head = far_row < far_heads
    far_block = jnp.where(far_head, far_row // HEAD, (far_row - far_heads) // TAIL)
    far_expert = (far_block // 2) * RUN + far_block % 2 + 2 * (1 - depth // 2)
    far_slot = jnp.where(far_head, far_row % HEAD, HEAD + far_row % TAIL)
    far_mix[...] = slots_of(far_expert, far_slot, far_both, far_counts, far_weights)[1].T.astype(BF16)

    for at in range(QUARTERS):
        wait_all(c_way, c_sems, at)
        unfold(at, c_rows, c_ext, unfold_all, rows, slots - rows)
        for half in range(2):
            part = dot_t(c_rows[:, columns(at)], down_w[half, at])
            rate_grad[half] = part if at == 0 else rate_grad[half] + part
    for half in range(2):
        gg[half] = (rate_grad[half] * der_gate[half]).astype(BF16)
        ug[half] = (rate_grad[half] * der_up[half]).astype(BF16)

    def dots_copy(step, there, landed_at):
        def tile(at):
            return pl.ds(pl.multiple_of(at * 8, 8), 8)

        return remote(
            dots.at[tile(there), :], dots_recv.at[tile(landed_at), :], v_send.at[step], v_recv.at[step], peer(step)
        )

    @pl.when(sec == 1)
    def _():
        for at in range(QUARTERS):
            value = dot_t(gg[0], gate_w[0, columns(at), :]) + dot_t(gg[1], gate_w[1, columns(at), :])
            value = value + dot_t(ug[0], up_w[0, columns(at), :]) + dot_t(ug[1], up_w[1, columns(at), :])
            store_slots(at, value * gain_ref[:, columns(at)], out_rows, out_ext)
            if at == 0:
                product = jnp.zeros((slots, 1), F32)
                for half in range(2):
                    terms = gg[half].astype(F32) * gate_act[half] + ug[half].astype(F32) * up_act[half]
                    product = product + jnp.sum(terms, axis=1, keepdims=True)
                placed = product * jnp.where(slot_at == iota((slots, tokens), 1), 1.0, 0.0)
                source_at = iota((8 * EXPERTS, slots), 1)
                source = jnp.where(source_at < rows, source_at // HEAD, (source_at - rows) // TAIL)
                group = jnp.where(source == iota((8 * EXPERTS, slots), 0) // 8, 1.0, 0.0)
                dots[...] = jnp.dot(
                    group, placed, precision=lax.Precision.HIGHEST, preferred_element_type=F32
                )

                def body(step, carry):
                    dots_copy(step, lax.rem(chip + step, EXPERTS), chip).start()
                    return carry

                lax.fori_loop(1, EXPERTS, body, 0)
                tile = pl.ds(pl.multiple_of(chip * 8, 8), 8)
                dots_recv[tile, :] = dots[tile, :]
            send_back(at)

    def sib_copy(step, at):
        part = pl.ds(pl.multiple_of(at * shard, shard), shard)
        return remote(sib_term.at[part, :], sib_recv.at[part, :], t_send.at[step], t_recv.at[step], sibling)

    def rep_copy(step, at):
        part = pl.ds(pl.multiple_of(at * shard, shard), shard)
        return remote(
            sib_recv.at[part, :], rep_recv.at[step - 1], r_send.at[step - 1], r_recv.at[step - 1], replica(step)
        )

    halves = shard // 2
    for step in range(n_dp + 1):
        if step < n_dp:
            at = lax.rem(dp + step + 1, n_dp)
            for piece in range(2):
                low = piece * halves
                part = pl.ds(pl.multiple_of(at * shard + low, halves), halves)
                own_term[step % 2, low : low + halves, :] = t_dot(x_rows[:, part], ug[core])
                sib_term[part, :] = t_dot(x_rows[:, part], ug[1 - core]).astype(BF16)
            sib_copy(step, at).start()
        if step > 0:
            at = lax.rem(dp + step, n_dp)
            sib_copy(step - 1, at).wait()
            part = pl.ds(pl.multiple_of(at * shard, shard), shard)
            sib_recv[part, :] = (own_term[(step - 1) % 2] + sib_recv[part, :].astype(F32)).astype(BF16)
            if step < n_dp:
                rep_copy(step, at).start()

    def pass_copy(at):
        return remote(
            final.at[:, columns(at)], landed.at[:, columns(at)], s_send.at[at], s_recv.at[at], across
        )

    def pass_on(at, base):
        wait_near(at)
        unfold(at, back_rows, back_ext, unfold_all, rows, slots - rows)
        final[:, columns(at)] = (base + dot(mix[...], back_rows[:, columns(at)])).astype(BF16)
        pass_copy(at).start()

    @pl.when(sec == 0)
    def _():
        for at in range(QUARTERS):
            pass_on(at, act_ref[:, columns(at)].astype(F32))

    @pl.when(sec == 1)
    def _():
        def body(step, carry):
            origin = lax.rem(chip + EXPERTS - step, EXPERTS)
            dots_copy(step, origin, origin).wait_recv()
            return carry

        lax.fori_loop(1, EXPERTS, body, 0)
        spread = jnp.where(
            expert_at[:, 0:1] * 8 == iota((slots, 8 * EXPERTS), 1), 1.0, 0.0
        )
        by_slot = jnp.dot(
            spread, dots_recv[...], precision=lax.Precision.HIGHEST, preferred_element_type=F32
        )
        product = jnp.sum(
            jnp.where(slot_at == iota((slots, tokens), 1), by_slot, 0.0), axis=1, keepdims=True
        )
        token_row = jnp.sum(taken * product, axis=0, keepdims=True)
        token_dot = jnp.sum(one * token_row, axis=1, keepdims=True)
        scale = inv_rms * inv_rms * token_dot / width
        for at in range(QUARTERS):
            cols = columns(at)
            pass_on(at, cot_ref[:, cols].astype(F32) - act_ref[:, cols].astype(F32) * scale)

    for step in range(1, n_dp):
        rep_copy(step, dp).wait_recv()
    own = pl.ds(pl.multiple_of(dp * shard, shard), shard)
    total_grad = sib_recv[own, :].astype(F32)
    for step in range(1, n_dp):
        total_grad = total_grad + rep_recv[step - 1].astype(F32)
    upgrad_ref[...] = total_grad.astype(BF16)

    edge = at_edge(depth)

    @pl.when(edge == 0)
    def _():
        for at in range(QUARTERS):
            pass_copy(at).wait()
            res_ref[:, columns(at)] = landed[:, columns(at)]

    @pl.when(edge == 1)
    def _():
        unfold_far = fold_order(far_blocks, False)
        for at in range(QUARTERS):
            wait_far(at)
            unfold(at, far_rows, far_ext, unfold_far, far_heads, far_slots - far_heads)
            direct = dot(far_mix[...], far_rows[:, columns(at)])
            pass_copy(at).wait()
            res_ref[:, columns(at)] = (landed[:, columns(at)].astype(F32) + direct).astype(BF16)

    wait_sent(x_way, x_sems)
    wait_sent(c_way, c_sems)
    wait_sent(b_way, b_sems)

    @pl.when(sec == 1)
    def _():
        def body(step, carry):
            dots_copy(step, lax.rem(chip + step, EXPERTS), chip).wait_send()
            return carry

        lax.fori_loop(1, EXPERTS, body, 0)

    for step in range(1, n_dp):
        rep_copy(step, dp).wait_send()


def per_device(
    activations, norm_gain, route_ids, route_gates, gate_weight, up_weight, leak_rates, down_weight, cotangent
):
    tokens, width = activations.shape[1:]
    hidden = gate_weight.shape[2]
    shard = down_weight.shape[2]
    n_dp = lax.axis_size("dp")
    rows = EXPERTS * HEAD
    slots = rows + EXPERTS * TAIL
    fold = width // FOLDS
    vmem = pl.BlockSpec(memory_space=pltpu.VMEM)
    anywhere = pl.BlockSpec(memory_space=pl.ANY)
    dma = pltpu.SemaphoreType.DMA

    def scratch(kind, *shape):
        return pltpu.VMEM(shape, kind)

    result, up_grad = pl.pallas_call(
        kernel,
        out_shape=(
            jax.ShapeDtypeStruct((tokens, width), BF16),
            jax.ShapeDtypeStruct((shard, hidden), BF16),
        ),
        in_specs=[vmem] * 6 + [anywhere] * 3,
        out_specs=(vmem, vmem),
        scratch_shapes=[
            scratch(BF16, 2, width, hidden),
            scratch(BF16, 2, width, hidden),
            scratch(BF16, 2, n_dp, hidden, shard),
            scratch(F32, 2, 8, hidden),
            scratch(BF16, rows, width),
            scratch(BF16, rows, fold),
            scratch(BF16, rows, width),
            scratch(BF16, rows, fold),
            scratch(BF16, slots, width),
            scratch(BF16, rows, fold),
            scratch(BF16, slots, width),
            scratch(BF16, rows, fold),
            scratch(F32, 2, slots, hidden),
            scratch(F32, 2, slots, hidden),
            scratch(BF16, 2, slots, hidden),
            scratch(F32, 2, slots, hidden),
            scratch(F32, 2, slots, hidden),
            scratch(F32, 2, slots, hidden),
            scratch(BF16, rows, width),
            scratch(BF16, rows, fold),
            scratch(BF16, slots, width),
            scratch(BF16, rows, fold),
            scratch(BF16, slots // 2, width),
            scratch(BF16, rows // 2, fold),
            scratch(BF16, tokens, width),
            scratch(BF16, tokens, width),
            scratch(F32, 8, tokens),
            scratch(F32, 8, tokens),
            scratch(F32, 8 * EXPERTS, tokens),
            scratch(F32, 8 * EXPERTS, tokens),
            scratch(BF16, tokens, slots),
            scratch(BF16, tokens, slots // 2),
            scratch(F32, 2, shard, hidden),
            scratch(BF16, width, hidden),
            scratch(BF16, width, hidden),
            scratch(BF16, n_dp - 1, shard, hidden),
            scratch(BF16, 2, slots, hidden),
            scratch(BF16, 2, slots, hidden),
            dma((4,)), dma((4,)), dma((4,)),
            dma((n_dp - 1,)), dma((n_dp - 1,)), dma((n_dp - 1,)), dma((n_dp - 1,)),
            *([dma((QUARTERS, 2 * EXPERTS))] * 6), dma((QUARTERS, EXPERTS)),
            dma((QUARTERS,)), dma((QUARTERS,)), dma((n_dp,)), dma((n_dp,)),
            dma((n_dp - 1,)), dma((n_dp - 1,)), dma((1,)), dma((1,)), dma((EXPERTS,)), dma((EXPERTS,)),
        ],
        compiler_params=pltpu.CompilerParams(
            collective_id=0, has_side_effects=True, vmem_limit_bytes=60 * 2**20
        ),
    )(
        activations[0],
        cotangent[0],
        norm_gain,
        route_ids[0].T,
        route_gates[0].T,
        jnp.broadcast_to(leak_rates, (8, hidden)),
        gate_weight[0],
        up_weight[0],
        down_weight[0],
    )
    first = lax.axis_index("section") == 0
    nothing = jnp.zeros_like(result)
    passed_on = jnp.where(first, nothing, result)
    passed_back = jnp.where(first, result, nothing)
    return (passed_on[None], passed_back[None], up_grad[None])


def solution(mesh):
    return jax.shard_map(
        per_device,
        mesh=mesh,
        in_specs=(
            P("section", ("dp", "expert"), None),
            P("section", None),
            P("section", ("dp", "expert"), None),
            P("section", ("dp", "expert"), None),
            P("section", None, "expert"),
            P("section", None, "expert"),
            P("section", "expert"),
            P("section", "expert", "dp"),
            P("section", ("dp", "expert"), None),
        ),
        out_specs=(
            P("section", ("dp", "expert"), None),
            P("section", ("dp", "expert"), None),
            P("section", "dp", "expert"),
        ),
        check_vma=False,
    )
```

```python
import functools

import jax
import jax.numpy as jnp
from jax import lax
from jax.experimental import pallas as pl
from jax.experimental.pallas import tpu as pltpu
from jax.sharding import PartitionSpec as P

MESH = pl.DeviceIdType.MESH
TSTEPS = 4
EPS = 1e-06
THETA = 0.5
SHARP = 4.0
HEAD = 16
TAIL = 2
FOLDS = 8
LANES = 128
QUARTERS = 4
EXPERTS = 16
RUN = 4
F32 = jnp.float32
BF16 = jnp.bfloat16


def iota(shape, dim):
    return lax.broadcasted_iota(jnp.int32, shape, dim)


def dot(a, b):
    return jnp.dot(a, b, preferred_element_type=F32)


def dot_t(a, b):
    return lax.dot_general(a, b, (((1,), (1,)), ((), ())), preferred_element_type=F32)


def t_dot(a, b):
    return lax.dot_general(a, b, (((0,), (0,)), ((), ())), preferred_element_type=F32)


def folds(value):
    return jnp.concatenate([value[:, at * LANES : (at + 1) * LANES] for at in range(FOLDS)], axis=0)


def fold_order(blocks, inverse):
    size = blocks * HEAD
    by_fold, by_block = iota((size, size), int(inverse)), iota((size, size), 1 - int(inverse))
    match = jnp.logical_and(
        by_fold // (blocks * TAIL) == (by_block % HEAD) // TAIL,
        jnp.logical_and(
            (by_fold % (blocks * TAIL)) // TAIL == by_block // HEAD, by_fold % TAIL == by_block % TAIL
        ),
    )
    return jnp.where(match, 1.0, 0.0).astype(BF16)


def routes(ids, tokens):
    named = iota((EXPERTS, tokens), 0).astype(F32)
    first = jnp.where(ids[0:1, :] == named, 1.0, 0.0)
    second = jnp.where(ids[1:2, :] == named, 1.0, 0.0)
    both = first + second
    earlier = jnp.where(iota((tokens, tokens), 0) < iota((tokens, tokens), 1), 1.0, 0.0)
    counts = dot(both.astype(BF16), earlier.astype(BF16))
    return first, second, both, counts


def slots_of(expert_at, slot_at, both, counts, weights):
    spread = jnp.where(expert_at[:, :EXPERTS] == iota((expert_at.shape[0], EXPERTS), 1), 1.0, 0.0)
    both_x = dot(spread.astype(BF16), both.astype(BF16))
    counts_x = dot(spread.astype(BF16), counts.astype(BF16))
    weights_x = jnp.dot(spread, weights, precision=lax.Precision.HIGHEST, preferred_element_type=F32)
    taken = both_x * jnp.where(counts_x == slot_at.astype(F32), 1.0, 0.0)
    return taken, taken * weights_x


def kernel(
    act_ref, cot_ref, gain_ref, ids_ref, gates_ref, leak_ref, gate_hbm, up_hbm, down_hbm,
    res_ref, upgrad_ref,
    gate_w, up_w, down_w, leak_w,
    send_x, send_c, x_rows, c_rows,
    gate_act, up_act, rate, der_gate, der_up, rate_grad,
    out_rows, back_rows, far_rows,
    final, landed, meta, meta_recv, dots, dots_recv, mix, far_mix,
    own_term, sib_term, sib_recv, rep_recv,
    gg, ug,
    w_own_sem, w_sib_send, w_sib_recv, d_send, d_recv, df_send, df_recv,
    x_send, x_recv, c_send, c_recv, b_send, b_recv, f_recv,
    s_send, s_recv, t_send, t_recv, r_send, r_recv, m_send, m_recv, v_send, v_recv,
):
    sec = lax.axis_index("section")
    dp = lax.axis_index("dp")
    lane = lax.axis_index("expert")
    n_dp = lax.axis_size("dp")
    chip = lane // 2
    core = lane % 2
    depth = chip % RUN
    tokens, width = act_ref.shape
    quarter = width // QUARTERS
    rows = EXPERTS * HEAD
    slots = rows + EXPERTS * TAIL
    hidden = gate_hbm.shape[1]
    shard = down_hbm.shape[1]
    far_blocks = EXPERTS // 2
    far_heads = far_blocks * HEAD
    far_slots = far_heads + far_blocks * TAIL

    def peer(step, section=sec):
        return (section, dp, lax.rem(chip + step, EXPERTS) * 2 + core)

    sibling = (sec, dp, chip * 2 + (1 - core))
    across = (1 - sec, dp, lane)

    def replica(step):
        return (sec, lax.rem(dp + step, n_dp), lane)

    def at_edge(place):
        return ((place + 1) // 2 + 1) % 2

    def is_far(home, expert):
        home_at, expert_at = home % RUN, expert % RUN
        return at_edge(home_at) * ((home_at // 2 + expert_at // 2) % 2)

    def remote(src, dst, send, recv, target):
        return pltpu.make_async_remote_copy(
            src_ref=src, dst_ref=dst, send_sem=send, recv_sem=recv,
            device_id=target, device_id_type=MESH,
        )

    barrier = pltpu.get_barrier_semaphore()

    def greet(step, carry):
        pl.semaphore_signal(barrier, inc=1, device_id=peer(step), device_id_type=MESH)
        return carry

    def greet_far(step, carry):
        there = lax.rem(chip + step, EXPERTS)

        @pl.when(is_far(there, chip) + is_far(chip, there) > 0)
        def _():
            pl.semaphore_signal(barrier, inc=1, device_id=peer(step, 1 - sec), device_id_type=MESH)

        return carry

    lax.fori_loop(1, EXPERTS, greet, 0)
    lax.fori_loop(1, EXPERTS, greet_far, 0)
    for step in range(1, n_dp):
        pl.semaphore_signal(barrier, inc=1, device_id=replica(step), device_id_type=MESH)
    pl.semaphore_signal(barrier, inc=1, device_id=sibling, device_id_type=MESH)
    pl.semaphore_signal(barrier, inc=1, device_id=across, device_id_type=MESH)

    ids = ids_ref[...].astype(F32)
    gates = gates_ref[...]
    first, second, both, counts = routes(ids, tokens)
    gate_of = first * gates[0:1, :] + second * gates[1:2, :]
    row_at = iota((slots, tokens), 0)
    in_head = row_at < rows
    expert_at = jnp.where(in_head, row_at // HEAD, (row_at - rows) // TAIL)
    slot_at = jnp.where(in_head, row_at % HEAD, HEAD + row_at % TAIL)
    taken, taken_gate = slots_of(expert_at, slot_at, both, counts, gate_of)
    slot_gate = jnp.sum(taken_gate, axis=1, keepdims=True)
    pick = taken.astype(BF16)
    fold_up = fold_order(EXPERTS, True)
    unfold_all = fold_order(EXPERTS, False)

    acts = act_ref[...].astype(F32)
    inv_rms = lax.rsqrt(jnp.mean(acts * acts, axis=-1, keepdims=True) + EPS)

    def columns(at):
        return slice(at * quarter, (at + 1) * quarter)

    pitch = quarter + LANES

    def heads(at):
        return slice(at * pitch, at * pitch + quarter)

    def tails(at):
        return slice(at * pitch + quarter, (at + 1) * pitch)

    def span(at):
        return slice(at * pitch, (at + 1) * pitch)

    def block(at):
        return pl.ds(pl.multiple_of(at * HEAD, HEAD), HEAD)

    def store_slots(at, value, ref):
        ref[0:rows, heads(at)] = value[0:rows].astype(BF16)
        ref[0:rows, tails(at)] = dot(fold_up, folds(value[rows:slots].astype(BF16))).astype(BF16)

    def unfold(at, ref, order, first_row, count):
        back = dot(order, ref[0:first_row, tails(at)]).astype(BF16)
        for fold in range(FOLDS):
            low = at * pitch + fold * LANES
            ref[first_row : first_row + count, low : low + LANES] = back[fold * count : (fold + 1) * count]

    def piece(way, sems, at, step, there, landed_at):
        src, dst = way
        send, recv = sems
        return remote(
            src.at[block(there), span(at)], dst.at[block(landed_at), span(at)], send.at[at], recv.at[at], peer(step)
        )

    def bulk(way, sems, at, blocks):
        src, dst = way
        send, recv = sems
        return remote(
            src.at[0 : blocks * HEAD, span(at)], dst.at[0 : blocks * HEAD, span(at)], send.at[at], recv.at[at], peer(1)
        )

    def send_all(way, sems, at):
        def body(step, carry):
            piece(way, sems, at, step, lax.rem(chip + step, EXPERTS), chip).start()
            return carry

        lax.fori_loop(1, EXPERTS, body, 0)

    def wait_all(way, sems, at):
        bulk(way, sems, at, EXPERTS - 1).wait_recv()

    def wait_sent(way, sems):
        for at in range(QUARTERS):
            bulk(way, sems, at, EXPERTS - 1).wait_send()

    def keep_own(way, at):
        src, dst = way
        dst[block(chip), span(at)] = src[block(chip), span(at)]

    x_way, x_sems = (send_x, x_rows), (x_send, x_recv)
    c_way, c_sems = (send_c, c_rows), (c_send, c_recv)
    b_way, b_sems = (out_rows, back_rows), (b_send, b_recv)

    own_weights = [
        pltpu.make_async_copy(gate_hbm, gate_w.at[core], w_own_sem.at[0]),
        pltpu.make_async_copy(up_hbm, up_w.at[core], w_own_sem.at[1]),
        pltpu.make_async_copy(down_hbm, down_w.at[core, dp], w_own_sem.at[2]),
        pltpu.make_async_copy(leak_ref, leak_w.at[core], w_own_sem.at[3]),
    ]

    def sib_weights(half):
        return [
            remote(gate_hbm, gate_w.at[half], w_sib_send.at[0], w_sib_recv.at[0], sibling),
            remote(up_hbm, up_w.at[half], w_sib_send.at[1], w_sib_recv.at[1], sibling),
            remote(down_hbm, down_w.at[half, dp], w_sib_send.at[2], w_sib_recv.at[2], sibling),
            remote(leak_ref, leak_w.at[half], w_sib_send.at[3], w_sib_recv.at[3], sibling),
        ]

    def down_copy(step, owner):
        return remote(
            down_hbm, down_w.at[core, owner], d_send.at[step - 1], d_recv.at[step - 1], replica(step)
        )

    def meta_copy():
        return remote(meta, meta_recv, m_send.at[0], m_recv.at[0], across)

    def prepare(at):
        cols = columns(at)
        normed = (act_ref[:, cols].astype(F32) * inv_rms * gain_ref[:, cols]).astype(BF16)
        store_slots(at, dot(pick, normed), send_x)

    prepare(0)
    pl.semaphore_wait(barrier, EXPERTS - 1 + n_dp - 1 + 2 + RUN + RUN * at_edge(depth))
    send_all(x_way, x_sems, 0)

    for copy in own_weights:
        copy.start()
    for copy in sib_weights(core):
        copy.start()
    for step in range(1, n_dp):
        down_copy(step, dp).start()

    for at in range(1, QUARTERS):
        prepare(at)
        send_all(x_way, x_sems, at)

    def send_grads(at):
        store_slots(at, dot(pick, cot_ref[:, columns(at)]) * slot_gate, send_c)
        send_all(c_way, c_sems, at)
        keep_own(c_way, at)

    for at in range(QUARTERS // 2):
        send_grads(at)
    for at in range(QUARTERS):
        keep_own(x_way, at)

    one = jnp.where(iota((tokens, tokens), 0) == iota((tokens, tokens), 1), 1.0, 0.0)
    inv_row = jnp.sum(one * inv_rms, axis=0, keepdims=True)
    is_first = sec == 0
    meta[...] = jnp.zeros_like(meta)
    meta[0:2, :] = ids
    meta[2:3, :] = jnp.where(is_first, gates[0:1, :], inv_row)
    meta[3:4, :] = jnp.where(is_first, gates[1:2, :], inv_row)
    meta_copy().start()

    differs = jnp.where((expert_at % RUN) // 2 == depth // 2, 0.0, 1.0) * at_edge(depth).astype(F32)
    mix[...] = (jnp.where(is_first, taken_gate, taken * inv_row) * (1.0 - differs)).T.astype(BF16)

    def clear(origin, carry):
        @pl.when(is_far(chip, origin) == 1)
        def _():
            back_rows[block(origin), :] = jnp.zeros((HEAD, QUARTERS * pitch), BF16)

        return carry

    lax.fori_loop(0, EXPERTS, clear, 0)

    for copy in own_weights:
        copy.wait()
    for copy in sib_weights(1 - core):
        copy.wait_recv()
    for copy in sib_weights(core):
        copy.wait_send()

    for at in range(QUARTERS):
        wait_all(x_way, x_sems, at)
        unfold(at, x_rows, unfold_all, rows, slots - rows)
        for half in range(2):
            for weight, total in ((gate_w, gate_act), (up_w, up_act)):
                part = dot(x_rows[:, heads(at)], weight[half, columns(at), :])
                total[half] = part if at == 0 else total[half] + part

    for half in range(2):

        def spiking(at, carry):
            part = pl.ds(pl.multiple_of(at * 32, 32), 32)
            gate_in = gate_act[half, part, :]
            up_in = up_act[half, part, :]
            leak = leak_w[half, 0:1, :]
            opened = lax.logistic(gate_in)
            silu = gate_in * opened
            drive = silu * up_in
            volts = drive
            volts_d = jnp.ones_like(drive)
            spike_sum = jnp.zeros_like(drive)
            spike_d = jnp.zeros_like(drive)
            for timestep in range(TSTEPS):
                if timestep:
                    volts = leak * volts + drive
                    volts_d = leak * volts_d + 1.0
                plus = lax.logistic(SHARP * (volts - THETA))
                minus = lax.logistic(SHARP * (-volts - THETA))
                spikes = plus - minus
                slope = SHARP * (plus * (1.0 - plus) + minus * (1.0 - minus))
                spikes_d = slope * volts_d
                volts = volts - THETA * spikes
                volts_d = volts_d - THETA * spikes_d
                spike_sum = spike_sum + spikes
                spike_d = spike_d + spikes_d
            rate[half, part, :] = (spike_sum / TSTEPS).astype(BF16)
            drive_d = spike_d / TSTEPS
            der_gate[half, part, :] = drive_d * up_in * (opened * (1.0 + gate_in * (1.0 - opened)))
            der_up[half, part, :] = drive_d * silu
            return carry

        lax.fori_loop(0, slots // 32, spiking, 0)

    def forward_down(step, half, owner):
        return remote(
            down_w.at[core, owner], down_w.at[half, owner],
            df_send.at[step - 1], df_recv.at[step - 1], sibling,
        )

    for step in range(1, n_dp):
        owner = lax.rem(dp + n_dp - step, n_dp)
        down_copy(step, owner).wait_recv()
        forward_down(step, core, owner).start()
    for step in range(1, n_dp):
        owner = lax.rem(dp + n_dp - step, n_dp)
        forward_down(step, 1 - core, owner).wait_recv()
        forward_down(step, core, owner).wait_send()
        down_copy(step, dp).wait_send()

    def far_place(origin):
        return (origin // RUN) * 2 + origin % 2

    def send_back(at):
        def body(step, carry):
            there = lax.rem(chip + step, EXPERTS)
            far = is_far(there, chip)

            @pl.when(far == 0)
            def _():
                piece(b_way, b_sems, at, step, there, chip).start()

            @pl.when(far == 1)
            def _():
                remote(
                    out_rows.at[block(there), span(at)], far_rows.at[block(far_place(chip)), span(at)],
                    b_send.at[at], f_recv.at[at], peer(step, 1 - sec),
                ).start()

            return carry

        lax.fori_loop(1, EXPERTS, body, 0)
        keep_own(b_way, at)

    def wait_near(at):
        @pl.when(at_edge(depth) == 0)
        def _():
            bulk(b_way, b_sems, at, EXPERTS - 1).wait_recv()

        @pl.when(at_edge(depth) == 1)
        def _():
            bulk(b_way, b_sems, at, EXPERTS - 1 - far_blocks).wait_recv()

    def wait_far(at):
        bulk((out_rows, far_rows), (b_send, f_recv), at, far_blocks).wait_recv()

    @pl.when(sec == 0)
    def _():
        for at in range(QUARTERS):
            value = dot(rate[0], down_w[0, at]) + dot(rate[1], down_w[1, at])
            store_slots(at, value, out_rows)
            send_back(at)

    for at in range(QUARTERS // 2, QUARTERS):
        send_grads(at)

    meta_copy().wait()
    far_first, far_second, far_both, far_counts = routes(meta_recv[0:2, :], tokens)
    far_weights = far_first * meta_recv[2:3, :] + far_second * meta_recv[3:4, :]
    far_row = iota((far_slots, tokens), 0)
    far_head = far_row < far_heads
    far_block = jnp.where(far_head, far_row // HEAD, (far_row - far_heads) // TAIL)
    far_expert = (far_block // 2) * RUN + far_block % 2 + 2 * (1 - depth // 2)
    far_slot = jnp.where(far_head, far_row % HEAD, HEAD + far_row % TAIL)
    far_mix[...] = slots_of(far_expert, far_slot, far_both, far_counts, far_weights)[1].T.astype(BF16)

    for at in range(QUARTERS):
        wait_all(c_way, c_sems, at)
        unfold(at, c_rows, unfold_all, rows, slots - rows)
        for half in range(2):
            part = dot_t(c_rows[:, heads(at)], down_w[half, at])
            rate_grad[half] = part if at == 0 else rate_grad[half] + part
    for half in range(2):
        gg[half] = (rate_grad[half] * der_gate[half]).astype(BF16)
        ug[half] = (rate_grad[half] * der_up[half]).astype(BF16)

    def dots_copy(step, there, landed_at):
        def tile(at):
            return pl.ds(pl.multiple_of(at * 8, 8), 8)

        return remote(
            dots.at[tile(there), :], dots_recv.at[tile(landed_at), :], v_send.at[0], v_recv.at[0], peer(step)
        )

    def dots_bulk():
        part = slice(0, 8 * (EXPERTS - 1))
        return remote(dots.at[part, :], dots_recv.at[part, :], v_send.at[0], v_recv.at[0], peer(1))

    @pl.when(sec == 1)
    def _():
        for at in range(QUARTERS):
            value = dot_t(gg[0], gate_w[0, columns(at), :]) + dot_t(gg[1], gate_w[1, columns(at), :])
            value = value + dot_t(ug[0], up_w[0, columns(at), :]) + dot_t(ug[1], up_w[1, columns(at), :])
            store_slots(at, value * gain_ref[:, columns(at)], out_rows)
            if at == 0:
                product = jnp.zeros((slots, 1), F32)
                for half in range(2):
                    terms = gg[half].astype(F32) * gate_act[half] + ug[half].astype(F32) * up_act[half]
                    product = product + jnp.sum(terms, axis=1, keepdims=True)
                placed = product * jnp.where(slot_at == iota((slots, tokens), 1), 1.0, 0.0)
                source_at = iota((8 * EXPERTS, slots), 1)
                source = jnp.where(source_at < rows, source_at // HEAD, (source_at - rows) // TAIL)
                group = jnp.where(source == iota((8 * EXPERTS, slots), 0) // 8, 1.0, 0.0)
                dots[...] = jnp.dot(
                    group, placed, precision=lax.Precision.HIGHEST, preferred_element_type=F32
                )

                def body(step, carry):
                    dots_copy(step, lax.rem(chip + step, EXPERTS), chip).start()
                    return carry

                lax.fori_loop(1, EXPERTS, body, 0)
                tile = pl.ds(pl.multiple_of(chip * 8, 8), 8)
                dots_recv[tile, :] = dots[tile, :]
            send_back(at)

    def sib_copy(step, at):
        part = pl.ds(pl.multiple_of(at * shard, shard), shard)
        return remote(sib_term.at[part, :], sib_recv.at[part, :], t_send.at[step], t_recv.at[step], sibling)

    def rep_copy(step, at):
        part = pl.ds(pl.multiple_of(at * shard, shard), shard)
        return remote(
            sib_recv.at[part, :], rep_recv.at[step - 1], r_send.at[step - 1], r_recv.at[step - 1], replica(step)
        )

    halves = shard // 2
    for step in range(n_dp + 1):
        if step < n_dp:
            at = lax.rem(dp + step + 1, n_dp)
            for piece in range(2):
                low = piece * halves
                part = pl.ds(pl.multiple_of(at * shard + low, halves), halves)
                normed = x_rows[:, pl.ds(pl.multiple_of(at * pitch + low, LANES), halves)]
                own_term[step % 2, low : low + halves, :] = t_dot(normed, ug[core])
                sib_term[part, :] = t_dot(normed, ug[1 - core]).astype(BF16)
            sib_copy(step, at).start()
        if step > 0:
            at = lax.rem(dp + step, n_dp)
            sib_copy(step - 1, at).wait()
            part = pl.ds(pl.multiple_of(at * shard, shard), shard)
            sib_recv[part, :] = (own_term[(step - 1) % 2] + sib_recv[part, :].astype(F32)).astype(BF16)
            if step < n_dp:
                rep_copy(step, at).start()

    def pass_copy(at):
        return remote(
            final.at[:, columns(at)], landed.at[:, columns(at)], s_send.at[at], s_recv.at[at], across
        )

    def pass_on(at, base):
        wait_near(at)
        unfold(at, back_rows, unfold_all, rows, slots - rows)
        final[:, columns(at)] = (base + dot(mix[...], back_rows[:, heads(at)])).astype(BF16)
        pass_copy(at).start()

    @pl.when(sec == 0)
    def _():
        for at in range(QUARTERS):
            pass_on(at, act_ref[:, columns(at)].astype(F32))

    @pl.when(sec == 1)
    def _():
        dots_bulk().wait_recv()
        spread = jnp.where(
            expert_at[:, 0:1] * 8 == iota((slots, 8 * EXPERTS), 1), 1.0, 0.0
        )
        by_slot = jnp.dot(
            spread, dots_recv[...], precision=lax.Precision.HIGHEST, preferred_element_type=F32
        )
        product = jnp.sum(
            jnp.where(slot_at == iota((slots, tokens), 1), by_slot, 0.0), axis=1, keepdims=True
        )
        token_row = jnp.sum(taken * product, axis=0, keepdims=True)
        token_dot = jnp.sum(one * token_row, axis=1, keepdims=True)
        scale = inv_rms * inv_rms * token_dot / width
        for at in range(QUARTERS):
            cols = columns(at)
            pass_on(at, cot_ref[:, cols].astype(F32) - act_ref[:, cols].astype(F32) * scale)

    for step in range(1, n_dp):
        rep_copy(step, dp).wait_recv()
    own = pl.ds(pl.multiple_of(dp * shard, shard), shard)
    total_grad = sib_recv[own, :].astype(F32)
    for step in range(1, n_dp):
        total_grad = total_grad + rep_recv[step - 1].astype(F32)
    upgrad_ref[...] = total_grad.astype(BF16)

    edge = at_edge(depth)

    @pl.when(edge == 0)
    def _():
        for at in range(QUARTERS):
            pass_copy(at).wait()
            res_ref[:, columns(at)] = landed[:, columns(at)]

    @pl.when(edge == 1)
    def _():
        unfold_far = fold_order(far_blocks, False)
        for at in range(QUARTERS):
            wait_far(at)
            unfold(at, far_rows, unfold_far, far_heads, far_slots - far_heads)
            direct = dot(far_mix[...], far_rows[:, heads(at)])
            pass_copy(at).wait()
            res_ref[:, columns(at)] = (landed[:, columns(at)].astype(F32) + direct).astype(BF16)

    wait_sent(x_way, x_sems)
    wait_sent(c_way, c_sems)
    wait_sent(b_way, b_sems)

    @pl.when(sec == 1)
    def _():
        dots_bulk().wait_send()

    for step in range(1, n_dp):
        rep_copy(step, dp).wait_send()


def per_device(
    activations, norm_gain, route_ids, route_gates, gate_weight, up_weight, leak_rates, down_weight, cotangent
):
    tokens, width = activations.shape[1:]
    hidden = gate_weight.shape[2]
    shard = down_weight.shape[2]
    n_dp = lax.axis_size("dp")
    rows = EXPERTS * HEAD
    slots = rows + EXPERTS * TAIL
    pitched = width + QUARTERS * LANES
    vmem = pl.BlockSpec(memory_space=pltpu.VMEM)
    anywhere = pl.BlockSpec(memory_space=pl.ANY)
    dma = pltpu.SemaphoreType.DMA

    def scratch(kind, *shape):
        return pltpu.VMEM(shape, kind)

    result, up_grad = pl.pallas_call(
        kernel,
        out_shape=(
            jax.ShapeDtypeStruct((tokens, width), BF16),
            jax.ShapeDtypeStruct((shard, hidden), BF16),
        ),
        in_specs=[vmem] * 6 + [anywhere] * 3,
        out_specs=(vmem, vmem),
        scratch_shapes=[
            scratch(BF16, 2, width, hidden),
            scratch(BF16, 2, width, hidden),
            scratch(BF16, 2, n_dp, hidden, shard),
            scratch(F32, 2, 8, hidden),
            scratch(BF16, rows, pitched),
            scratch(BF16, rows, pitched),
            scratch(BF16, slots, pitched),
            scratch(BF16, slots, pitched),
            scratch(F32, 2, slots, hidden),
            scratch(F32, 2, slots, hidden),
            scratch(BF16, 2, slots, hidden),
            scratch(F32, 2, slots, hidden),
            scratch(F32, 2, slots, hidden),
            scratch(F32, 2, slots, hidden),
            scratch(BF16, rows, pitched),
            scratch(BF16, slots, pitched),
            scratch(BF16, slots // 2, pitched),
            scratch(BF16, tokens, width),
            scratch(BF16, tokens, width),
            scratch(F32, 8, tokens),
            scratch(F32, 8, tokens),
            scratch(F32, 8 * EXPERTS, tokens),
            scratch(F32, 8 * EXPERTS, tokens),
            scratch(BF16, tokens, slots),
            scratch(BF16, tokens, slots // 2),
            scratch(F32, 2, shard, hidden),
            scratch(BF16, width, hidden),
            scratch(BF16, width, hidden),
            scratch(BF16, n_dp - 1, shard, hidden),
            scratch(BF16, 2, slots, hidden),
            scratch(BF16, 2, slots, hidden),
            dma((4,)), dma((4,)), dma((4,)),
            dma((n_dp - 1,)), dma((n_dp - 1,)), dma((n_dp - 1,)), dma((n_dp - 1,)),
            *([dma((QUARTERS,))] * 7),
            dma((QUARTERS,)), dma((QUARTERS,)), dma((n_dp,)), dma((n_dp,)),
            dma((n_dp - 1,)), dma((n_dp - 1,)), dma((1,)), dma((1,)), dma((1,)), dma((1,)),
        ],
        compiler_params=pltpu.CompilerParams(
            collective_id=0, has_side_effects=True, vmem_limit_bytes=60 * 2**20
        ),
    )(
        activations[0],
        cotangent[0],
        norm_gain,
        route_ids[0].T,
        route_gates[0].T,
        jnp.broadcast_to(leak_rates, (8, hidden)),
        gate_weight[0],
        up_weight[0],
        down_weight[0],
    )
    first = lax.axis_index("section") == 0
    nothing = jnp.zeros_like(result)
    passed_on = jnp.where(first, nothing, result)
    passed_back = jnp.where(first, result, nothing)
    return (passed_on[None], passed_back[None], up_grad[None])


def solution(mesh):
    return jax.shard_map(
        per_device,
        mesh=mesh,
        in_specs=(
            P("section", ("dp", "expert"), None),
            P("section", None),
            P("section", ("dp", "expert"), None),
            P("section", ("dp", "expert"), None),
            P("section", None, "expert"),
            P("section", None, "expert"),
            P("section", "expert"),
            P("section", "expert", "dp"),
            P("section", ("dp", "expert"), None),
        ),
        out_specs=(
            P("section", ("dp", "expert"), None),
            P("section", ("dp", "expert"), None),
            P("section", "dp", "expert"),
        ),
        check_vma=False,
    )
```

```python
import functools

import jax
import jax.numpy as jnp
from jax import lax
from jax.experimental import pallas as pl
from jax.experimental.pallas import tpu as pltpu
from jax.sharding import PartitionSpec as P

MESH = pl.DeviceIdType.MESH
TSTEPS = 4
EPS = 1e-06
THETA = 0.5
SHARP = 4.0
HEAD = 16
TAIL = 2
FOLDS = 8
LANES = 128
QUARTERS = 4
GROUPS = 2
EXPERTS = 16
RUN = 4
F32 = jnp.float32
BF16 = jnp.bfloat16


def iota(shape, dim):
    return lax.broadcasted_iota(jnp.int32, shape, dim)


def dot(a, b):
    return jnp.dot(a, b, preferred_element_type=F32)


def dot_t(a, b):
    return lax.dot_general(a, b, (((1,), (1,)), ((), ())), preferred_element_type=F32)


def t_dot(a, b):
    return lax.dot_general(a, b, (((0,), (0,)), ((), ())), preferred_element_type=F32)


def folds(value):
    return jnp.concatenate([value[:, at * LANES : (at + 1) * LANES] for at in range(FOLDS)], axis=0)


def fold_order(blocks, inverse):
    size = blocks * HEAD
    by_fold, by_block = iota((size, size), int(inverse)), iota((size, size), 1 - int(inverse))
    match = jnp.logical_and(
        by_fold // (blocks * TAIL) == (by_block % HEAD) // TAIL,
        jnp.logical_and(
            (by_fold % (blocks * TAIL)) // TAIL == by_block // HEAD, by_fold % TAIL == by_block % TAIL
        ),
    )
    return jnp.where(match, 1.0, 0.0).astype(BF16)


def routes(ids, tokens):
    named = iota((EXPERTS, tokens), 0).astype(F32)
    first = jnp.where(ids[0:1, :] == named, 1.0, 0.0)
    second = jnp.where(ids[1:2, :] == named, 1.0, 0.0)
    both = first + second
    earlier = jnp.where(iota((tokens, tokens), 0) < iota((tokens, tokens), 1), 1.0, 0.0)
    counts = dot(both.astype(BF16), earlier.astype(BF16))
    return first, second, both, counts


def slots_of(expert_at, slot_at, both, counts, weights):
    spread = jnp.where(expert_at[:, :EXPERTS] == iota((expert_at.shape[0], EXPERTS), 1), 1.0, 0.0)
    both_x = dot(spread.astype(BF16), both.astype(BF16))
    counts_x = dot(spread.astype(BF16), counts.astype(BF16))
    weights_x = jnp.dot(spread, weights, precision=lax.Precision.HIGHEST, preferred_element_type=F32)
    taken = both_x * jnp.where(counts_x == slot_at.astype(F32), 1.0, 0.0)
    return taken, taken * weights_x


def kernel(
    gain_ref, ids_ref, gates_ref, act_hbm, cot_hbm, leak_hbm, gate_hbm, up_hbm, down_hbm,
    passed_on_hbm, passed_back_hbm, up_grad_hbm,
    act_ref, cot_ref, nothing,
    gate_w, up_w, down_w, leak_w,
    send_x, send_c, x_rows, c_rows,
    gate_act, up_act, rate, der_gate, der_up, rate_grad,
    out_rows, back_rows, far_rows,
    final, landed, meta, meta_recv, dots, dots_recv, mix, far_mix,
    own_term, sib_term, sib_recv, rep_recv,
    gg, ug,
    w_own_sem, w_sib_send, w_sib_recv, d_send, d_recv, df_send, df_recv,
    x_send, x_recv, c_send, c_recv, b_send, b_recv, f_recv,
    s_send, s_recv, t_send, t_recv, r_send, r_recv, m_send, m_recv, v_send, v_recv,
    in_sem, out_sem,
):
    sec = lax.axis_index("section")
    dp = lax.axis_index("dp")
    lane = lax.axis_index("expert")
    n_dp = lax.axis_size("dp")
    chip = lane // 2
    core = lane % 2
    depth = chip % RUN
    tokens, width = act_ref.shape
    quarter = width // QUARTERS
    rows = EXPERTS * HEAD
    slots = rows + EXPERTS * TAIL
    hidden = gate_hbm.shape[1]
    shard = down_hbm.shape[1]
    far_blocks = EXPERTS // 2
    far_heads = far_blocks * HEAD
    far_slots = far_heads + far_blocks * TAIL

    def peer(step, section=sec):
        return (section, dp, lax.rem(chip + step, EXPERTS) * 2 + core)

    sibling = (sec, dp, chip * 2 + (1 - core))
    across = (1 - sec, dp, lane)

    def replica(step):
        return (sec, lax.rem(dp + step, n_dp), lane)

    def at_edge(place):
        return ((place + 1) // 2 + 1) % 2

    def is_far(home, expert):
        home_at, expert_at = home % RUN, expert % RUN
        return at_edge(home_at) * ((home_at // 2 + expert_at // 2) % 2)

    def remote(src, dst, send, recv, target):
        return pltpu.make_async_remote_copy(
            src_ref=src, dst_ref=dst, send_sem=send, recv_sem=recv,
            device_id=target, device_id_type=MESH,
        )

    act_in = pltpu.make_async_copy(act_hbm, act_ref, in_sem.at[0])
    cot_in = pltpu.make_async_copy(cot_hbm, cot_ref, in_sem.at[1])
    act_in.start()
    barrier = pltpu.get_barrier_semaphore()

    def greet(step, carry):
        pl.semaphore_signal(barrier, inc=1, device_id=peer(step), device_id_type=MESH)
        return carry

    def greet_far(step, carry):
        there = lax.rem(chip + step, EXPERTS)

        @pl.when(is_far(there, chip) + is_far(chip, there) > 0)
        def _():
            pl.semaphore_signal(barrier, inc=1, device_id=peer(step, 1 - sec), device_id_type=MESH)

        return carry

    lax.fori_loop(1, EXPERTS, greet, 0)
    lax.fori_loop(1, EXPERTS, greet_far, 0)
    for step in range(1, n_dp):
        pl.semaphore_signal(barrier, inc=1, device_id=replica(step), device_id_type=MESH)
    pl.semaphore_signal(barrier, inc=1, device_id=sibling, device_id_type=MESH)
    pl.semaphore_signal(barrier, inc=1, device_id=across, device_id_type=MESH)

    ids = ids_ref[...].astype(F32)
    gates = gates_ref[...]
    first, second, both, counts = routes(ids, tokens)
    gate_of = first * gates[0:1, :] + second * gates[1:2, :]
    row_at = iota((slots, tokens), 0)
    in_head = row_at < rows
    expert_at = jnp.where(in_head, row_at // HEAD, (row_at - rows) // TAIL)
    slot_at = jnp.where(in_head, row_at % HEAD, HEAD + row_at % TAIL)
    taken, taken_gate = slots_of(expert_at, slot_at, both, counts, gate_of)
    slot_gate = jnp.sum(taken_gate, axis=1, keepdims=True)
    pick = taken.astype(BF16)
    fold_up = fold_order(EXPERTS, True)
    unfold_all = fold_order(EXPERTS, False)
    per_group = EXPERTS // GROUPS
    group_heads = per_group * HEAD
    group_rows = slots // GROUPS
    fold_group = fold_order(per_group, True)
    unfold_group = fold_order(per_group, False)

    act_in.wait()
    cot_in.start()
    acts = act_ref[...].astype(F32)
    inv_rms = lax.rsqrt(jnp.mean(acts * acts, axis=-1, keepdims=True) + EPS)

    def columns(at):
        return slice(at * quarter, (at + 1) * quarter)

    pitch = quarter + LANES

    def heads(at):
        return slice(at * pitch, at * pitch + quarter)

    def tails(at):
        return slice(at * pitch + quarter, (at + 1) * pitch)

    def span(at):
        return slice(at * pitch, (at + 1) * pitch)

    def block(at):
        return pl.ds(pl.multiple_of(at * HEAD, HEAD), HEAD)

    def spot(step):
        return pl.ds(pl.multiple_of((step // per_group) * group_rows + (step % per_group) * HEAD, HEAD), HEAD)

    def group(at):
        return slice(at * group_rows, (at + 1) * group_rows)

    def store_group(which, at, value, ref):
        part = slice(which * group_heads, (which + 1) * group_heads)
        ref[part, heads(at)] = value[0:group_heads].astype(BF16)
        ref[part, tails(at)] = dot(fold_group, folds(value[group_heads:group_rows].astype(BF16))).astype(BF16)

    def store_slots(at, value, ref):
        ref[0:rows, heads(at)] = value[0:rows].astype(BF16)
        ref[0:rows, tails(at)] = dot(fold_up, folds(value[rows:slots].astype(BF16))).astype(BF16)

    def unfold(at, ref, order, first_row, count, base=0):
        back = dot(order, ref[base : base + first_row, tails(at)]).astype(BF16)
        start = base + first_row
        for fold in range(FOLDS):
            low = at * pitch + fold * LANES
            ref[start : start + count, low : low + LANES] = back[fold * count : (fold + 1) * count]

    def unfold_slots(which, at, ref):
        unfold(at, ref, unfold_group, group_heads, group_rows - group_heads, which * group_rows)

    def piece(way, sems, at, sem_at, source, target, step):
        src, dst = way
        send, recv = sems
        return remote(
            src.at[source, span(at)], dst.at[target, span(at)], send.at[sem_at], recv.at[sem_at], peer(step)
        )

    def bulk(way, sems, at, sem_at, blocks):
        part = slice(0, blocks * HEAD)
        return piece(way, sems, at, sem_at, part, part, 1)

    def send_out(way, sems, at, sem_at, low, high):
        def body(step, carry):
            there = lax.rem(chip + step, EXPERTS)
            piece(way, sems, at, sem_at, block(there), spot(step), step).start()
            return carry

        lax.fori_loop(low, high, body, 0)

    def keep_own(way, at):
        src, dst = way
        dst[spot(0), span(at)] = src[block(chip), span(at)]

    x_way, x_sems = (send_x, x_rows), (x_send, x_recv)
    c_way, c_sems = (send_c, c_rows), (c_send, c_recv)
    b_way, b_sems = (out_rows, back_rows), (b_send, b_recv)

    def either(start, copy_first, copy_second):
        @pl.when(sec == 0)
        def _():
            copy_first.start() if start else copy_first.wait()

        @pl.when(sec == 1)
        def _():
            copy_second.start() if start else copy_second.wait()

    def result_out(at, start):
        cols = columns(at)
        either(
            start,
            pltpu.make_async_copy(landed.at[:, cols], passed_back_hbm.at[:, cols], out_sem.at[1 + at]),
            pltpu.make_async_copy(landed.at[:, cols], passed_on_hbm.at[:, cols], out_sem.at[1 + at]),
        )

    def zeros_out(at, start):
        cols = columns(at)
        sem = out_sem.at[1 + QUARTERS + at]
        either(
            start,
            pltpu.make_async_copy(nothing, passed_on_hbm.at[:, cols], sem),
            pltpu.make_async_copy(nothing, passed_back_hbm.at[:, cols], sem),
        )

    own_weights = [
        pltpu.make_async_copy(gate_hbm, gate_w.at[core], w_own_sem.at[0]),
        pltpu.make_async_copy(up_hbm, up_w.at[core], w_own_sem.at[1]),
        pltpu.make_async_copy(down_hbm, down_w.at[core, dp], w_own_sem.at[2]),
        pltpu.make_async_copy(leak_hbm, leak_w.at[core], w_own_sem.at[3]),
    ]

    def sib_weights(half):
        return [
            remote(gate_hbm, gate_w.at[half], w_sib_send.at[0], w_sib_recv.at[0], sibling),
            remote(up_hbm, up_w.at[half], w_sib_send.at[1], w_sib_recv.at[1], sibling),
            remote(down_hbm, down_w.at[half, dp], w_sib_send.at[2], w_sib_recv.at[2], sibling),
            remote(leak_hbm, leak_w.at[half], w_sib_send.at[3], w_sib_recv.at[3], sibling),
        ]

    def down_copy(step, owner):
        return remote(
            down_hbm, down_w.at[core, owner], d_send.at[step - 1], d_recv.at[step - 1], replica(step)
        )

    def meta_copy():
        return remote(meta, meta_recv, m_send.at[0], m_recv.at[0], across)

    def prepare(at):
        cols = columns(at)
        normed = (act_ref[:, cols].astype(F32) * inv_rms * gain_ref[:, cols]).astype(BF16)
        store_slots(at, dot(pick, normed), send_x)

    prepare(0)
    pl.semaphore_wait(barrier, EXPERTS - 1 + n_dp - 1 + 2 + RUN + RUN * at_edge(depth))
    send_out(x_way, x_sems, 0, 0, 1, EXPERTS)

    for copy in own_weights:
        copy.start()
    for copy in sib_weights(core):
        copy.start()
    for step in range(1, n_dp):
        down_copy(step, dp).start()

    for at in range(1, QUARTERS):
        prepare(at)
        send_out(x_way, x_sems, at, at, 1, EXPERTS)

    cot_in.wait()

    group_steps = [(max(1, which * per_group), (which + 1) * per_group) for which in range(GROUPS)]
    for at in range(QUARTERS):
        store_slots(at, dot(pick, cot_ref[:, columns(at)]) * slot_gate, send_c)
        send_out(c_way, c_sems, at, at, *group_steps[0])
    for at in range(QUARTERS):
        send_out(c_way, c_sems, at, QUARTERS + at, *group_steps[1])
    for at in range(QUARTERS):
        keep_own(x_way, at)
        keep_own(c_way, at)

    one = jnp.where(iota((tokens, tokens), 0) == iota((tokens, tokens), 1), 1.0, 0.0)
    inv_row = jnp.sum(one * inv_rms, axis=0, keepdims=True)
    is_first = sec == 0
    meta[...] = jnp.zeros_like(meta)
    meta[0:2, :] = ids
    meta[2:3, :] = jnp.where(is_first, gates[0:1, :], inv_row)
    meta[3:4, :] = jnp.where(is_first, gates[1:2, :], inv_row)
    meta_copy().start()

    differs = jnp.where((expert_at % RUN) // 2 == depth // 2, 0.0, 1.0) * at_edge(depth).astype(F32)
    mix[...] = (jnp.where(is_first, taken_gate, taken * inv_row) * (1.0 - differs)).T.astype(BF16)

    def clear(origin, carry):
        @pl.when(is_far(chip, origin) == 1)
        def _():
            back_rows[block(origin), :] = jnp.zeros((HEAD, QUARTERS * pitch), BF16)

        return carry

    lax.fori_loop(0, EXPERTS, clear, 0)

    nothing[...] = jnp.zeros_like(nothing)
    for at in range(QUARTERS):
        zeros_out(at, True)

    for copy in own_weights:
        copy.wait()
    for copy in sib_weights(1 - core):
        copy.wait_recv()
    for copy in sib_weights(core):
        copy.wait_send()

    for at in range(QUARTERS):
        bulk(x_way, x_sems, at, at, EXPERTS - 1).wait_recv()
        for which in range(GROUPS):
            unfold_slots(which, at, x_rows)
        for half in range(2):
            for weight, total in ((gate_w, gate_act), (up_w, up_act)):
                part = dot(x_rows[:, heads(at)], weight[half, columns(at), :])
                total[half] = part if at == 0 else total[half] + part

    for half in range(2):

        def spiking(at, carry):
            part = pl.ds(pl.multiple_of(at * 32, 32), 32)
            gate_in = gate_act[half, part, :]
            up_in = up_act[half, part, :]
            leak = leak_w[half]
            opened = lax.logistic(gate_in)
            silu = gate_in * opened
            drive = silu * up_in
            volts = drive
            volts_d = jnp.ones_like(drive)
            spike_sum = jnp.zeros_like(drive)
            spike_d = jnp.zeros_like(drive)
            for timestep in range(TSTEPS):
                if timestep:
                    volts = leak * volts + drive
                    volts_d = leak * volts_d + 1.0
                plus = lax.logistic(SHARP * (volts - THETA))
                minus = lax.logistic(SHARP * (-volts - THETA))
                spikes = plus - minus
                slope = SHARP * (plus * (1.0 - plus) + minus * (1.0 - minus))
                spikes_d = slope * volts_d
                volts = volts - THETA * spikes
                volts_d = volts_d - THETA * spikes_d
                spike_sum = spike_sum + spikes
                spike_d = spike_d + spikes_d
            rate[half, part, :] = (spike_sum / TSTEPS).astype(BF16)
            drive_d = spike_d / TSTEPS
            der_gate[half, part, :] = drive_d * up_in * (opened * (1.0 + gate_in * (1.0 - opened)))
            der_up[half, part, :] = drive_d * silu
            return carry

        lax.fori_loop(0, slots // 32, spiking, 0)

    def forward_down(step, half, owner):
        return remote(
            down_w.at[core, owner], down_w.at[half, owner],
            df_send.at[step - 1], df_recv.at[step - 1], sibling,
        )

    for step in range(1, n_dp):
        owner = lax.rem(dp + n_dp - step, n_dp)
        down_copy(step, owner).wait_recv()
        forward_down(step, core, owner).start()
    for step in range(1, n_dp):
        owner = lax.rem(dp + n_dp - step, n_dp)
        forward_down(step, 1 - core, owner).wait_recv()
        forward_down(step, core, owner).wait_send()
        down_copy(step, dp).wait_send()

    def far_place(origin):
        return (origin // RUN) * 2 + origin % 2

    def send_back(which, at):
        def body(step, carry):
            turn = EXPERTS - step
            far = is_far(lax.rem(chip + turn, EXPERTS), chip)

            @pl.when(far == 0)
            def _():
                piece(b_way, b_sems, at, at, block(step), block(chip), turn).start()

            @pl.when(far == 1)
            def _():
                remote(
                    out_rows.at[block(step), span(at)], far_rows.at[block(far_place(chip)), span(at)],
                    b_send.at[at], f_recv.at[at], peer(turn, 1 - sec),
                ).start()

            return carry

        lax.fori_loop(*group_steps[which], body, 0)
        if which == 0:
            back_rows[block(chip), span(at)] = out_rows[0:HEAD, span(at)]

    def wait_near(at):
        @pl.when(at_edge(depth) == 0)
        def _():
            bulk(b_way, b_sems, at, at, EXPERTS - 1).wait_recv()

        @pl.when(at_edge(depth) == 1)
        def _():
            bulk(b_way, b_sems, at, at, EXPERTS - 1 - far_blocks).wait_recv()

    def wait_far(at):
        bulk((out_rows, far_rows), (b_send, f_recv), at, at, far_blocks).wait_recv()

    @pl.when(sec == 0)
    def _():
        for at in range(QUARTERS):
            value = dot(rate[0], down_w[0, at]) + dot(rate[1], down_w[1, at])
            for which in range(GROUPS):
                store_group(which, at, value[group(which)], out_rows)
                send_back(which, at)

    meta_copy().wait()
    far_first, far_second, far_both, far_counts = routes(meta_recv[0:2, :], tokens)
    far_weights = far_first * meta_recv[2:3, :] + far_second * meta_recv[3:4, :]
    far_row = iota((far_slots, tokens), 0)
    far_head = far_row < far_heads
    far_block = jnp.where(far_head, far_row // HEAD, (far_row - far_heads) // TAIL)
    far_expert = (far_block // 2) * RUN + far_block % 2 + 2 * (1 - depth // 2)
    far_slot = jnp.where(far_head, far_row % HEAD, HEAD + far_row % TAIL)
    far_mix[...] = slots_of(far_expert, far_slot, far_both, far_counts, far_weights)[1].T.astype(BF16)

    def dots_copy(turn, source, target):
        return remote(dots.at[source, :], dots_recv.at[target, :], v_send.at[0], v_recv.at[0], peer(turn))

    def tile(at):
        return pl.ds(pl.multiple_of(at * 8, 8), 8)

    def dots_bulk():
        part = slice(0, 8 * (EXPERTS - 1))
        return dots_copy(1, part, part)

    def send_dots():
        product = jnp.zeros((slots, 1), F32)
        for half in range(2):
            terms = gg[half].astype(F32) * gate_act[half] + ug[half].astype(F32) * up_act[half]
            product = product + jnp.sum(terms, axis=1, keepdims=True)
        local_row = iota((slots, tokens), 0) % group_rows
        local_slot = jnp.where(local_row < group_heads, local_row % HEAD, HEAD + local_row % TAIL)
        placed = product * jnp.where(local_slot == iota((slots, tokens), 1), 1.0, 0.0)
        column = iota((8 * EXPERTS, slots), 1)
        within = column % group_rows
        source = jnp.where(within < group_heads, within // HEAD, (within - group_heads) // TAIL)
        source = source + (column // group_rows) * per_group
        gather = jnp.where(source == iota((8 * EXPERTS, slots), 0) // 8, 1.0, 0.0)
        dots[...] = jnp.dot(gather, placed, precision=lax.Precision.HIGHEST, preferred_element_type=F32)

        def body(step, carry):
            dots_copy(EXPERTS - step, tile(step), tile(chip)).start()
            return carry

        lax.fori_loop(1, EXPERTS, body, 0)
        dots_recv[tile(chip), :] = dots[0:8, :]

    for which in range(GROUPS):
        part = group(which)
        for at in range(QUARTERS):
            low, high = group_steps[which]
            bulk(c_way, c_sems, at, which * QUARTERS + at, high - low).wait_recv()
            unfold_slots(which, at, c_rows)
            for half in range(2):
                term = dot_t(c_rows[part, heads(at)], down_w[half, at])
                rate_grad[half, part, :] = term if at == 0 else rate_grad[half, part, :] + term
        for half in range(2):
            gg[half, part, :] = (rate_grad[half, part, :] * der_gate[half, part, :]).astype(BF16)
            ug[half, part, :] = (rate_grad[half, part, :] * der_up[half, part, :]).astype(BF16)

        @pl.when(sec == 1)
        def _():
            for at in range(QUARTERS):
                cols = columns(at)
                value = dot_t(gg[0, part, :], gate_w[0, cols, :]) + dot_t(gg[1, part, :], gate_w[1, cols, :])
                value = value + dot_t(ug[0, part, :], up_w[0, cols, :]) + dot_t(ug[1, part, :], up_w[1, cols, :])
                store_group(which, at, value * gain_ref[:, cols], out_rows)
                send_back(which, at)
                if which == GROUPS - 1 and at == 0:
                    send_dots()

    def sib_copy(step, at):
        part = pl.ds(pl.multiple_of(at * shard, shard), shard)
        return remote(sib_term.at[part, :], sib_recv.at[part, :], t_send.at[step], t_recv.at[step], sibling)

    def rep_copy(step, at):
        part = pl.ds(pl.multiple_of(at * shard, shard), shard)
        return remote(
            sib_recv.at[part, :], rep_recv.at[step - 1], r_send.at[step - 1], r_recv.at[step - 1], replica(step)
        )

    halves = shard // 2
    for step in range(n_dp + 1):
        if step < n_dp:
            at = lax.rem(dp + step + 1, n_dp)
            for side in range(2):
                low = side * halves
                part = pl.ds(pl.multiple_of(at * shard + low, halves), halves)
                normed = x_rows[:, pl.ds(pl.multiple_of(at * pitch + low, LANES), halves)]
                own_term[step % 2, low : low + halves, :] = t_dot(normed, ug[core])
                sib_term[part, :] = t_dot(normed, ug[1 - core]).astype(BF16)
            sib_copy(step, at).start()
        if step > 0:
            at = lax.rem(dp + step, n_dp)
            sib_copy(step - 1, at).wait()
            part = pl.ds(pl.multiple_of(at * shard, shard), shard)
            sib_recv[part, :] = (own_term[(step - 1) % 2] + sib_recv[part, :].astype(F32)).astype(BF16)
            if step < n_dp:
                rep_copy(step, at).start()

    def pass_copy(at):
        return remote(
            final.at[:, columns(at)], landed.at[:, columns(at)], s_send.at[at], s_recv.at[at], across
        )

    def pass_on(at, base):
        wait_near(at)
        unfold(at, back_rows, unfold_all, rows, slots - rows)
        final[:, columns(at)] = (base + dot(mix[...], back_rows[:, heads(at)])).astype(BF16)
        pass_copy(at).start()

    @pl.when(sec == 0)
    def _():
        for at in range(QUARTERS):
            pass_on(at, act_ref[:, columns(at)].astype(F32))

    @pl.when(sec == 1)
    def _():
        dots_bulk().wait_recv()
        spread = jnp.where(
            expert_at[:, 0:1] * 8 == iota((slots, 8 * EXPERTS), 1), 1.0, 0.0
        )
        by_slot = jnp.dot(
            spread, dots_recv[...], precision=lax.Precision.HIGHEST, preferred_element_type=F32
        )
        product = jnp.sum(
            jnp.where(slot_at == iota((slots, tokens), 1), by_slot, 0.0), axis=1, keepdims=True
        )
        token_row = jnp.sum(taken * product, axis=0, keepdims=True)
        token_dot = jnp.sum(one * token_row, axis=1, keepdims=True)
        scale = inv_rms * inv_rms * token_dot / width
        for at in range(QUARTERS):
            cols = columns(at)
            pass_on(at, cot_ref[:, cols].astype(F32) - act_ref[:, cols].astype(F32) * scale)

    for step in range(1, n_dp):
        rep_copy(step, dp).wait_recv()
    own = pl.ds(pl.multiple_of(dp * shard, shard), shard)
    total_grad = sib_recv[own, :].astype(F32)
    for step in range(1, n_dp):
        total_grad = total_grad + rep_recv[step - 1].astype(F32)
    sib_recv[own, :] = total_grad.astype(BF16)
    grad_out = pltpu.make_async_copy(sib_recv.at[own, :], up_grad_hbm, out_sem.at[0])
    grad_out.start()

    edge = at_edge(depth)

    @pl.when(edge == 0)
    def _():
        for at in range(QUARTERS):
            pass_copy(at).wait()
            result_out(at, True)

    @pl.when(edge == 1)
    def _():
        unfold_far = fold_order(far_blocks, False)
        for at in range(QUARTERS):
            wait_far(at)
            unfold(at, far_rows, unfold_far, far_heads, far_slots - far_heads)
            direct = dot(far_mix[...], far_rows[:, heads(at)])
            pass_copy(at).wait()
            landed[:, columns(at)] = (landed[:, columns(at)].astype(F32) + direct).astype(BF16)
            result_out(at, True)

    for at in range(QUARTERS):
        zeros_out(at, False)
        result_out(at, False)
    grad_out.wait()
    for at in range(QUARTERS):
        bulk(x_way, x_sems, at, at, EXPERTS - 1).wait_send()
        bulk(b_way, b_sems, at, at, EXPERTS - 1).wait_send()
        for which, (low, high) in enumerate(group_steps):
            bulk(c_way, c_sems, at, which * QUARTERS + at, high - low).wait_send()

    @pl.when(sec == 1)
    def _():
        dots_bulk().wait_send()

    for step in range(1, n_dp):
        rep_copy(step, dp).wait_send()


def per_device(
    activations, norm_gain, route_ids, route_gates, gate_weight, up_weight, leak_rates, down_weight, cotangent
):
    tokens, width = activations.shape[1:]
    hidden = gate_weight.shape[2]
    shard = down_weight.shape[2]
    n_dp = lax.axis_size("dp")
    rows = EXPERTS * HEAD
    slots = rows + EXPERTS * TAIL
    pitched = width + QUARTERS * LANES
    vmem = pl.BlockSpec(memory_space=pltpu.VMEM)
    anywhere = pl.BlockSpec(memory_space=pl.ANY)
    dma = pltpu.SemaphoreType.DMA

    def scratch(kind, *shape):
        return pltpu.VMEM(shape, kind)

    passed_on, passed_back, up_grad = pl.pallas_call(
        kernel,
        out_shape=(
            jax.ShapeDtypeStruct((tokens, width), BF16),
            jax.ShapeDtypeStruct((tokens, width), BF16),
            jax.ShapeDtypeStruct((shard, hidden), BF16),
        ),
        in_specs=[vmem] * 3 + [anywhere] * 6,
        out_specs=(anywhere, anywhere, anywhere),
        scratch_shapes=[
            scratch(BF16, tokens, width),
            scratch(BF16, tokens, width),
            scratch(BF16, tokens, width // QUARTERS),
            scratch(BF16, 2, width, hidden),
            scratch(BF16, 2, width, hidden),
            scratch(BF16, 2, n_dp, hidden, shard),
            scratch(F32, 2, 1, hidden),
            scratch(BF16, rows, pitched),
            scratch(BF16, rows, pitched),
            scratch(BF16, slots, pitched),
            scratch(BF16, slots, pitched),
            scratch(F32, 2, slots, hidden),
            scratch(F32, 2, slots, hidden),
            scratch(BF16, 2, slots, hidden),
            scratch(F32, 2, slots, hidden),
            scratch(F32, 2, slots, hidden),
            scratch(F32, 2, slots, hidden),
            scratch(BF16, rows, pitched),
            scratch(BF16, slots, pitched),
            scratch(BF16, slots // 2, pitched),
            scratch(BF16, tokens, width),
            scratch(BF16, tokens, width),
            scratch(F32, 8, tokens),
            scratch(F32, 8, tokens),
            scratch(F32, 8 * EXPERTS, tokens),
            scratch(F32, 8 * EXPERTS, tokens),
            scratch(BF16, tokens, slots),
            scratch(BF16, tokens, slots // 2),
            scratch(F32, 2, shard, hidden),
            scratch(BF16, width, hidden),
            scratch(BF16, width, hidden),
            scratch(BF16, n_dp - 1, shard, hidden),
            scratch(BF16, 2, slots, hidden),
            scratch(BF16, 2, slots, hidden),
            dma((4,)), dma((4,)), dma((4,)),
            dma((n_dp - 1,)), dma((n_dp - 1,)), dma((n_dp - 1,)), dma((n_dp - 1,)),
            *([dma((QUARTERS,))] * 2), *([dma((GROUPS * QUARTERS,))] * 2), *([dma((QUARTERS,))] * 3),
            dma((QUARTERS,)), dma((QUARTERS,)), dma((n_dp,)), dma((n_dp,)),
            dma((n_dp - 1,)), dma((n_dp - 1,)), dma((1,)), dma((1,)), dma((1,)), dma((1,)),
            dma((2,)), dma((1 + 2 * QUARTERS,)),
        ],
        compiler_params=pltpu.CompilerParams(
            collective_id=0, has_side_effects=True, vmem_limit_bytes=60 * 2**20
        ),
    )(
        norm_gain,
        route_ids[0].T,
        route_gates[0].T,
        activations[0],
        cotangent[0],
        leak_rates,
        gate_weight[0],
        up_weight[0],
        down_weight[0],
    )
    return (passed_on[None], passed_back[None], up_grad[None])


def solution(mesh):
    return jax.shard_map(
        per_device,
        mesh=mesh,
        in_specs=(
            P("section", ("dp", "expert"), None),
            P("section", None),
            P("section", ("dp", "expert"), None),
            P("section", ("dp", "expert"), None),
            P("section", None, "expert"),
            P("section", None, "expert"),
            P("section", "expert"),
            P("section", "expert", "dp"),
            P("section", ("dp", "expert"), None),
        ),
        out_specs=(
            P("section", ("dp", "expert"), None),
            P("section", ("dp", "expert"), None),
            P("section", "dp", "expert"),
        ),
        check_vma=False,
    )
```
